512 devices in a mesh: tm: 32 (over z, core), chan: 16 (over y, x).
Axes of the slice: x: 4, y: 4, z: 16, core: 2. Of those that a mesh axis runs over, the one named last changes fastest.
Arguments:
- latent: bfloat16 [384, 96, 416], P('chan', 'tm'), may hold values from -50 to 50
- norm_gain_one: float32 [384], P('chan'), may hold values from 0.1 to 1.9
- conv_weight_one: bfloat16 [3, 9, 384, 384], P(None, None, 'chan'), may hold values from -0.5 to 0.5
- conv_bias_one: float32 [384], P('chan'), may hold values from -3 to 3
- norm_gain_two: float32 [384], P('chan'), may hold values from 0.1 to 1.9
- conv_weight_two: bfloat16 [3, 9, 384, 384], P(None, None, 'chan'), may hold values from -0.5 to 0.5
- conv_bias_two: float32 [384], P('chan'), may hold values from -3 to 3
Outputs:
- block_out: bfloat16 [384, 96, 416], P('chan', 'tm')
The draws below stay inside these ranges and needn't reach their ends.
All inputs are finite; a program needn't handle non-finite values.
Results may differ from the reference program's by a relative error of at most 0.0059.
Values may be sent and summed in bfloat16 or wider, within the bound.
A program may use at most 64 MiB of HBM per device.

```python
import math
import jax
import jax.numpy as jnp
from jax import lax

C = 384
COLS = 104
ROWS = 4
PIX = 416
FRAMES = 96


def draw_latent(key, part):
    key = jax.random.fold_in(key, 11)
    key_chan, key_cell, key_base, key_common = jax.random.split(key, 4)
    index = jnp.arange(C, dtype=jnp.float32)
    chan_scale = jnp.exp((index / C - 0.5) * math.log(3.0) + jax.random.uniform(key_chan, (C,), jnp.float32, -0.55, 0.55))
    cell_scale = jnp.exp(jax.random.uniform(key_cell, (FRAMES, PIX), jnp.float32, math.log(0.3), math.log(3.0)))
    base = jax.random.normal(key_base, (C, FRAMES, PIX), jnp.float32)
    base = base + jax.random.normal(key_common, (1, FRAMES, PIX), jnp.float32)
    base = jnp.clip(base, -5.0, 5.0)
    return (base * chan_scale[:, None, None] * cell_scale[None]).astype(jnp.bfloat16)


def shared_weight(key):
    key_rand, key_tap, key_in, key_out = jax.random.split(key, 4)
    spread = (27.0 * C) ** (-0.5)
    randpart = jnp.clip(jax.random.normal(key_rand, (3, 9, C, C), jnp.float32), -4.0, 4.0) * spread
    tap_factor = jnp.clip(jax.random.normal(key_tap, (3, 9), jnp.float32), -2.5, 2.5)
    in_pattern = jax.random.uniform(key_in, (C,), jnp.float32, 0.5, 1.5)
    out_pattern = jnp.clip(jax.random.normal(key_out, (C,), jnp.float32), -2.5, 2.5)
    common = 0.4 / C * tap_factor[:, :, None, None] * in_pattern[None, None, :, None] * out_pattern[None, None, None, :]
    return (randpart + common).astype(jnp.bfloat16)


def draw_conv_weight_one(key, part):
    key = jax.random.fold_in(key, 23)
    return shared_weight(key)


def draw_conv_weight_two(key, part):
    key = jax.random.fold_in(key, 37)
    return shared_weight(key)


def levels(own_key, extent, shards, least, top_value):
    def one(axis_at, shards_of):
        draws = jax.random.uniform(jax.random.fold_in(jax.random.fold_in(own_key, 6), axis_at), (shards_of,), jnp.float32, least / len(shards), top_value / len(shards))
        return jnp.repeat(jnp.exp(draws), extent[axis_at] // shards_of).reshape((-1,) + (1,) * (len(extent) - axis_at - 1))

    factor_of = one(*shards[0])
    for cut in shards[1:]:
        factor_of = factor_of * one(*cut)
    return factor_of


def normal_values(stream_key, dims, scale, limit, cuts=(), kind=jnp.bfloat16):
    values = scale * jax.random.normal(stream_key, dims, jnp.float32)
    if cuts:
        values = values * levels(stream_key, dims, cuts, -0.22, 0.18)
    return jnp.clip(values, -limit, limit).astype(kind)


def setup_inputs(seed: int = 0) -> dict:
    streams_of = jax.random.split(jax.random.key(seed), 8)
    latent = draw_latent(jax.random.fold_in(streams_of[7], 71), 0)
    norm_gain_one = jnp.clip(1.0 + 0.18 * jax.random.normal(streams_of[1], (C,), jnp.float32), 0.1, 1.9)
    conv_weight_one = draw_conv_weight_one(jax.random.fold_in(streams_of[7], 71), 0)
    conv_bias_one = normal_values(streams_of[3], (C,), 0.5, 3.0, ((0, 16),), jnp.float32)
    norm_gain_two = jnp.clip(1.0 + 0.18 * jax.random.normal(streams_of[4], (C,), jnp.float32), 0.1, 1.9)
    conv_weight_two = draw_conv_weight_two(jax.random.fold_in(streams_of[7], 71), 0)
    conv_bias_two = normal_values(streams_of[6], (C,), 0.5, 3.0, ((0, 16),), jnp.float32)
    return {"latent": latent, "norm_gain_one": norm_gain_one, "conv_weight_one": conv_weight_one, "conv_bias_one": conv_bias_one, "norm_gain_two": norm_gain_two, "conv_weight_two": conv_weight_two, "conv_bias_two": conv_bias_two}


def activate(value, gain):
    v32 = value.astype(jnp.float32)
    mean_sq = lax.optimization_barrier(jnp.mean(v32 * v32, axis=0, keepdims=True))
    normed = v32 * lax.rsqrt(mean_sq + 1e-06) * gain[:, None, None]
    return jax.nn.silu(normed).astype(jnp.bfloat16)

def spatial_stack(act):
    chans, frames, cells = act.shape
    grid = act.reshape(chans, frames, ROWS, COLS)
    padded = jnp.pad(grid, ((0, 0), (0, 0), (1, 1), (1, 1)))
    pieces = []
    for dy in range(3):
        for dx in range(3):
            pieces.append(padded[:, :, dy:dy + ROWS, dx:dx + COLS].reshape(chans, frames, cells))
    return jnp.stack(pieces, 0)

def convolve(act, weight, bias):
    frames = act.shape[1]
    padded = jnp.pad(act, ((0, 0), (2, 0), (0, 0)))
    stacked = spatial_stack(padded).astype(jnp.float32)
    weight32 = weight.astype(jnp.float32)
    total = jnp.zeros((weight.shape[3], frames, act.shape[2]), jnp.float32)
    for k in range(3):
        total = total + jnp.einsum('sco,scfp->ofp', weight32[k], stacked[:, :, k:k + frames])
    return total + bias[:, None, None]

def reference(latent, norm_gain_one, conv_weight_one, conv_bias_one, norm_gain_two, conv_weight_two, conv_bias_two):
    first = activate(latent, norm_gain_one)
    middle = convolve(first, conv_weight_one, conv_bias_one).astype(jnp.bfloat16)
    second = activate(middle, norm_gain_two)
    result = latent.astype(jnp.float32) + convolve(second, conv_weight_two, conv_bias_two)
    return result.astype(jnp.bfloat16)
```

```python
import functools

import jax
import jax.numpy as jnp
from jax import lax
from jax.experimental import pallas as pl
from jax.experimental.pallas import tpu as pltpu
from jax.sharding import PartitionSpec as P

COLS = 104
ROWS = 4
LANES = 128
WIDE = ROWS * LANES
SIDE = 4
OWN = 24
HALF = WIDE // 2
DEPTH = 256
F32 = jnp.float32
BF16 = jnp.bfloat16


def unfold(value):
    value = value.astype(F32)
    return jnp.concatenate([value[:OWN], value[OWN:]], axis=1)


def fold(value):
    return jnp.concatenate([value[:, :HALF], value[:, HALF:]], axis=0).astype(BF16)


def tile4(value):
    return jnp.concatenate([value] * ROWS, axis=1)


def lane_ids(rows):
    return lax.broadcasted_iota(jnp.int32, (rows, LANES), 1)


def spread(frame):
    flat = jnp.concatenate([frame, jnp.zeros((OWN, WIDE - ROWS * COLS), F32)], axis=1)
    lane = lane_ids(OWN)
    rows = []
    for row in range(ROWS):
        at, off = divmod(row * COLS, LANES)
        piece = flat[:, at * LANES : (at + 1) * LANES]
        if off:
            after = flat[:, (at + 1) * LANES : (at + 2) * LANES]
            piece = jnp.where(
                lane < LANES - off,
                pltpu.roll(piece, LANES - off, 1),
                pltpu.roll(after, LANES - off, 1),
            )
        rows.append(jnp.where(lane < COLS, piece, 0.0))
    return jnp.concatenate(rows, axis=1)


def squeeze(frame):
    lane = lane_ids(OWN)
    rows = [frame[:, r * LANES : (r + 1) * LANES] for r in range(ROWS)]
    pieces = []
    for at in range(ROWS):
        row, off = divmod(at * LANES, COLS)
        piece = rows[row]
        if off:
            piece = pltpu.roll(piece, LANES - off, 1)
        if row + 1 < ROWS:
            piece = jnp.where(lane < COLS - off, piece, pltpu.roll(rows[row + 1], COLS - off, 1))
        pieces.append(piece)
    return jnp.concatenate(pieces, axis=1)[:, : ROWS * COLS]


def kernel(
    sections,
    chans,
    lat_hbm,
    w1_hbm,
    w2_hbm,
    g1_hbm,
    b1_hbm,
    g2_hbm,
    b2_hbm,
    out_ref,
    lat,
    weights,
    vecs,
    flipped,
    gains,
    values,
    partial_a,
    partial_b,
    w_out,
    w_in,
    stacked,
    sums,
    own_sums,
    shares,
    from_line,
    from_before,
    local_sem,
    gain_send,
    gain_recv,
    value_send,
    value_recv,
    pa_send,
    pa_recv,
    pb_send,
    pb_recv,
    w_send,
    w_recv,
    line_send,
    line_recv,
    next_send,
    next_recv,
):
    t = lax.axis_index("tm")
    chan = lax.axis_index("chan")
    x, y = lax.rem(chan, SIDE), lax.div(chan, SIDE)
    parity = lax.rem(t, 2)

    swap = [parity, 1 - parity]
    index_a = [x + s * (y - x) for s in swap]
    index_b = [y + s * (x - y) for s in swap]

    def chan_at(j, a, b):
        s = swap[j]
        return a * (1 + (SIDE - 1) * s) + b * (SIDE - (SIDE - 1) * s)

    def shifted(index, d):
        return lax.rem(index + d, SIDE)

    def a_peer(j, d):
        return (t, chan_at(j, shifted(index_a[j], d), index_b[j]))

    def b_peer(j, d, later=0):
        return (t + later, chan_at(j, index_a[j], shifted(index_b[j], d)))

    def remote(src, dst, send, recv, device):
        return pltpu.make_async_remote_copy(
            src_ref=src,
            dst_ref=dst,
            send_sem=send,
            recv_sem=recv,
            device_id=device,
            device_id_type=pl.DeviceIdType.MESH,
        )

    far_first = (2, 1, 3)

    loads = [
        pltpu.make_async_copy(lat_hbm, lat, local_sem.at[0]),
        pltpu.make_async_copy(w1_hbm, weights.at[0], local_sem.at[1]),
        pltpu.make_async_copy(w2_hbm, weights.at[1], local_sem.at[2]),
    ]
    for n, ref in enumerate((g1_hbm, b1_hbm, g2_hbm, b2_hbm)):
        loads.append(pltpu.make_async_copy(ref, vecs.at[n], local_sem.at[3 + n]))
    for load in loads:
        load.start()

    barrier = pltpu.get_barrier_semaphore()

    def greet(device):
        pl.semaphore_signal(barrier, inc=1, device_id=device, device_id_type=pl.DeviceIdType.MESH)

    for d in range(1, SIDE):
        greet((t, SIDE * y + shifted(x, d)))
        greet((t, SIDE * shifted(y, d) + x))

    @pl.when(t > 0)
    def _():
        greet((t - 1, chan))
        for d in range(1, SIDE):
            greet((t - 1, SIDE * y + shifted(x, d)))
            greet((t - 1, SIDE * shifted(y, d) + x))

    def own_squares(j, f, value):
        squares = jnp.sum(value * value, axis=0, keepdims=True)
        partial_a[j, 0, 2 * f : 2 * f + 1, :] = squares[:, :HALF]
        partial_a[j, 0, 2 * f + 1 : 2 * f + 2, :] = squares[:, HALF:]

    for j in range(2):
        partial_a[j, 0] = jnp.zeros((8, HALF), F32)
    loads[0].wait()
    for f in range(3):
        value = spread(lat[f].astype(F32))
        values[0, 0, f] = fold(value)
        own_squares(0, f, value)

    for n in range(4):
        loads[3 + n].wait()
    lane = lane_ids(8)
    flipped[...] = jnp.zeros((LANES, LANES), F32)
    for n in range(4):
        flipped[n : n + 1, 0:OWN] = vecs[n]
    columns = jnp.transpose(flipped[...])[:OWN]

    def column(n):
        return jnp.broadcast_to(columns[:, n : n + 1], (OWN, LANES))

    bias = [column(1), column(3)]
    gains[0, 0] = column(0)
    gains[1, 0] = column(2)

    pl.semaphore_wait(barrier, 2 * (SIDE - 1) + jnp.where(t < sections - 1, 2 * SIDE - 1, 0))

    sends = []

    def start(copy):
        copy.start()
        sends.append(copy)

    def send_squares_a(j):
        for d in far_first:
            start(
                remote(
                    partial_a.at[j, 0],
                    partial_a.at[j, SIDE - d],
                    pa_send.at[j, d],
                    pa_recv.at[j, SIDE - d],
                    b_peer(j, d),
                )
            )

    def send_values(j):
        for d in far_first:
            start(
                remote(
                    values.at[j, 0],
                    values.at[j, SIDE - d],
                    value_send.at[j, d],
                    value_recv.at[j, SIDE - d],
                    a_peer(j, d),
                )
            )

    def send_squares_b(j):
        total = partial_a[j, 0]
        for d in (1, 3, 2):
            remote(
                partial_a.at[j, 0], partial_a.at[j, d], pa_send.at[j, d], pa_recv.at[j, d], b_peer(j, d)
            ).wait_recv()
            total = total + partial_a[j, d]
        partial_b[j, 0] = total
        for d in far_first:
            start(
                remote(
                    partial_b.at[j, 0],
                    partial_b.at[j, SIDE - d],
                    pb_send.at[j, d],
                    pb_recv.at[j, SIDE - d],
                    a_peer(j, d),
                )
            )

    def scales(j):
        total = partial_b[j, 0]
        for d in (1, 3, 2):
            remote(
                partial_b.at[j, 0], partial_b.at[j, d], pb_send.at[j, d], pb_recv.at[j, d], a_peer(j, d)
            ).wait_recv()
            total = total + partial_b[j, d]
        return lax.rsqrt(total / chans + 1e-06)

    def turn_weights(j):
        loads[1 + j].wait()
        for k in range(3):
            part = weights[j, 9 * k : 9 * k + 9].astype(F32).reshape(9 * OWN, chans)
            part = jnp.concatenate([part, jnp.zeros((DEPTH - 9 * OWN, chans), F32)], axis=0)
            flat = jnp.transpose(part)
            sums[0:chans, 0:DEPTH] = flat
            for d in range(SIDE):
                rows = []
                for e in range(SIDE):
                    block = chan_at(j, shifted(index_a[j], d), shifted(index_b[j], e))
                    rows.append(sums[pl.ds(pl.multiple_of(block * OWN, 8), OWN), 0:DEPTH])
                rows = jnp.concatenate(rows, axis=0).astype(BF16)
                if d == 0:
                    w_in[j, 0, k] = rows
                else:
                    w_out[j, d - 1, k] = rows

    def send_weights(j):
        for d in far_first:
            start(
                remote(
                    w_out.at[j, d - 1],
                    w_in.at[j, SIDE - d],
                    w_send.at[j, d],
                    w_recv.at[j, SIDE - d],
                    a_peer(j, d),
                )
            )

    def send_gains(j):
        for d in far_first:
            start(
                remote(
                    gains.at[j, 0],
                    gains.at[j, SIDE - d],
                    gain_send.at[j, d],
                    gain_recv.at[j, SIDE - d],
                    a_peer(j, d),
                )
            )

    def stack_taps(slot, j, scale):
        gain = tile4(gains[j, slot])
        for f in range(3):
            value = unfold(values[j, slot, f])
            row = jnp.concatenate([scale[2 * f : 2 * f + 1], scale[2 * f + 1 : 2 * f + 2]], axis=1)
            normed = value * row * gain
            act = 0.5 * normed * (1.0 + jnp.tanh(0.5 * normed))
            act = act.astype(BF16).astype(F32)
            rows = [act[:, r * LANES : (r + 1) * LANES] for r in range(ROWS)]
            shifts = [
                [pltpu.roll(r, 1, 1) for r in rows],
                rows,
                [pltpu.roll(r, LANES - 1, 1) for r in rows],
            ]
            none = jnp.zeros((OWN, LANES), F32)
            taps = []
            for dy in range(3):
                for dx in range(3):
                    moved = [none] + shifts[dx] + [none]
                    taps.append(jnp.concatenate(moved[dy : dy + ROWS], axis=1))
            taps.append(jnp.zeros((DEPTH - 9 * OWN, WIDE), F32))
            stacked[f, slot] = jnp.concatenate(taps, axis=0).astype(BF16)

    def convolve(j):
        left = jnp.concatenate([w_in[j, s].reshape(3 * SIDE * OWN, DEPTH) for s in range(SIDE)], axis=1)
        group = SIDE * OWN

        def emit(frame, total):
            for e in range(SIDE):
                piece = total[e * OWN : (e + 1) * OWN]
                if e == 0 and frame < 3:
                    own_sums[frame] = piece
                else:
                    shares[j, e, frame] = fold(piece)

        def product(f):
            return jnp.dot(left, stacked[f].reshape(SIDE * DEPTH, WIDE), preferred_element_type=F32)

        last = product(2)
        emit(4, last[:group])
        sums[0:group, :] = last[group : 2 * group]
        sums[group : 2 * group, :] = last[2 * group :]
        mid = product(1)
        emit(3, sums[0:group, :] + mid[:group])
        sums[group : 2 * group, :] += mid[group : 2 * group]
        sums[0:group, :] = mid[2 * group :]

        @pl.when(t < sections - 1)
        def _():
            for e in range(SIDE):
                next_copy(j, e).start()

        first = product(0)
        emit(2, sums[group : 2 * group, :] + first[:group])
        emit(1, sums[0:group, :] + first[group : 2 * group])
        emit(0, first[2 * group :])
        for d in far_first:
            start(line_copy(j, d))

    def next_copy(j, e):
        return remote(
            shares.at[j, e, pl.ds(3, 2)],
            from_before.at[j, e],
            next_send.at[j, e],
            next_recv.at[j, e],
            b_peer(j, e, 1),
        )

    def line_copy(j, d):
        return remote(
            shares.at[j, d, pl.ds(0, 3)],
            from_line.at[j, SIDE - d],
            line_send.at[j, d],
            line_recv.at[j, SIDE - d],
            b_peer(j, d),
        )

    def collect(j):
        @pl.when(t > 0)
        def _():
            for e in range(SIDE):
                remote(
                    from_before.at[j, e],
                    from_before.at[j, e],
                    next_send.at[j, e],
                    next_recv.at[j, e],
                    (t, chan_at(j, shifted(index_a[j], 1), index_b[j])),
                ).wait_recv()

        for d in (1, 3, 2):
            remote(
                from_line.at[j, d],
                from_line.at[j, d],
                line_send.at[j, d],
                line_recv.at[j, d],
                b_peer(j, d),
            ).wait_recv()
        frames = []
        for f in range(3):
            total = own_sums[f] + tile4(bias[j])
            for d in range(1, SIDE):
                total = total + unfold(from_line[j, d, f])
            if f < 2:
                for e in range(SIDE):
                    total = total + unfold(from_before[j, e, f])
            frames.append(total)
        return frames

    @pl.when(t == 0)
    def _():
        from_before[...] = jnp.zeros(from_before.shape, BF16)

    send_squares_a(0)
    send_values(0)
    send_gains(0)
    send_gains(1)
    turn_weights(0)
    send_weights(0)
    send_squares_b(0)
    turn_weights(1)
    scale = scales(0)
    for slot in (0, 1, 3, 2):
        if slot:
            remote(
                values.at[0, 0], values.at[0, slot], value_send.at[0, slot], value_recv.at[0, slot], a_peer(0, slot)
            ).wait_recv()
            remote(
                gains.at[0, 0], gains.at[0, slot], gain_send.at[0, slot], gain_recv.at[0, slot], a_peer(0, slot)
            ).wait_recv()
        stack_taps(slot, 0, scale)
    for slot in (1, 3, 2):
        remote(
            w_out.at[0, 0], w_in.at[0, slot], w_send.at[0, slot], w_recv.at[0, slot], a_peer(0, slot)
        ).wait_recv()
    send_weights(1)
    convolve(0)

    frames = collect(0)
    keep = tile4(lane_ids(OWN)) < COLS
    for f in range(3):
        middle = jnp.where(keep, frames[f], 0.0).astype(BF16).astype(F32)
        values[1, 0, f] = fold(middle)
        own_squares(1, f, middle)
    send_squares_a(1)
    send_values(1)
    send_squares_b(1)
    scale = scales(1)
    for slot in (0, 1, 3, 2):
        if slot:
            remote(
                gains.at[1, 0], gains.at[1, slot], gain_send.at[1, slot], gain_recv.at[1, slot], a_peer(1, slot)
            ).wait_recv()
            remote(
                values.at[1, 0], values.at[1, slot], value_send.at[1, slot], value_recv.at[1, slot], a_peer(1, slot)
            ).wait_recv()
        stack_taps(slot, 1, scale)
    for slot in (1, 3, 2):
        remote(
            w_out.at[1, 0], w_in.at[1, slot], w_send.at[1, slot], w_recv.at[1, slot], a_peer(1, slot)
        ).wait_recv()
    convolve(1)
    frames = collect(1)
    for f in range(3):
        out_ref[f] = (lat[f].astype(F32) + squeeze(frames[f])).astype(BF16)

    for copy in sends:
        copy.wait_send()

    @pl.when(t < sections - 1)
    def _():
        for j in range(2):
            for e in range(SIDE):
                next_copy(j, e).wait_send()


def block(sections, latent, gain_one, weight_one, bias_one, gain_two, weight_two, bias_two):
    frames = latent.shape[1]
    chans = weight_one.shape[3]
    dma = pltpu.SemaphoreType.DMA
    anywhere = pl.BlockSpec(memory_space=pl.ANY)
    result = pl.pallas_call(
        functools.partial(kernel, sections, chans),
        out_shape=jax.ShapeDtypeStruct((frames, OWN, ROWS * COLS), BF16),
        in_specs=[anywhere] * 7,
        out_specs=pl.BlockSpec(memory_space=pltpu.VMEM),
        scratch_shapes=[
            pltpu.VMEM((frames, OWN, ROWS * COLS), BF16),
            pltpu.VMEM((2, 27, OWN, chans), BF16),
            pltpu.VMEM((4, 1, OWN), F32),
            pltpu.VMEM((LANES, LANES), F32),
            pltpu.VMEM((2, SIDE, OWN, LANES), F32),
            pltpu.VMEM((2, SIDE, frames, 2 * OWN, HALF), BF16),
            pltpu.VMEM((2, SIDE, 8, HALF), F32),
            pltpu.VMEM((2, SIDE, 8, HALF), F32),
            pltpu.VMEM((2, SIDE - 1, 3, SIDE * OWN, DEPTH), BF16),
            pltpu.VMEM((2, SIDE, 3, SIDE * OWN, DEPTH), BF16),
            pltpu.VMEM((frames, SIDE, DEPTH, WIDE), BF16),
            pltpu.VMEM((chans, WIDE), F32),
            pltpu.VMEM((frames, OWN, WIDE), F32),
            pltpu.VMEM((2, SIDE, frames + 2, 2 * OWN, HALF), BF16),
            pltpu.VMEM((2, SIDE, frames, 2 * OWN, HALF), BF16),
            pltpu.VMEM((2, SIDE, 2, 2 * OWN, HALF), BF16),
            dma((7,)),
        ]
        + [dma((2, SIDE))] * 14,
        compiler_params=pltpu.CompilerParams(
            collective_id=0, has_side_effects=True, vmem_limit_bytes=40 * 1024 * 1024
        ),
    )(
        jnp.transpose(latent, (1, 0, 2)),
        weight_one.reshape(27, OWN, chans),
        weight_two.reshape(27, OWN, chans),
        gain_one.reshape(1, OWN),
        bias_one.reshape(1, OWN),
        gain_two.reshape(1, OWN),
        bias_two.reshape(1, OWN),
    )
    return jnp.transpose(result, (1, 0, 2))


def solution(mesh):
    in_specs = (
        P("chan", "tm", None),
        P("chan"),
        P(None, None, "chan", None),
        P("chan"),
        P("chan"),
        P(None, None, "chan", None),
        P("chan"),
    )
    return jax.shard_map(
        functools.partial(block, mesh.shape["tm"]),
        mesh=mesh,
        in_specs=in_specs,
        out_specs=P("chan", "tm", None),
        check_vma=False,
    )
```

```python
import functools

import jax
import jax.numpy as jnp
from jax import lax
from jax.experimental import pallas as pl
from jax.experimental.pallas import tpu as pltpu
from jax.sharding import PartitionSpec as P

COLS = 104
ROWS = 4
LANES = 128
WIDE = ROWS * LANES
SIDE = 4
OWN = 24
HALF = WIDE // 2
DEPTH = 256
F32 = jnp.float32
BF16 = jnp.bfloat16


def unfold(value):
    value = value.astype(F32)
    return jnp.concatenate([value[:OWN], value[OWN:]], axis=1)


def fold(value):
    return jnp.concatenate([value[:, :HALF], value[:, HALF:]], axis=0).astype(BF16)


def tile4(value):
    return jnp.concatenate([value] * ROWS, axis=1)


def lane_ids(rows):
    return lax.broadcasted_iota(jnp.int32, (rows, LANES), 1)


def spread(frame):
    flat = jnp.concatenate([frame, jnp.zeros((OWN, WIDE - ROWS * COLS), F32)], axis=1)
    lane = lane_ids(OWN)
    rows = []
    for row in range(ROWS):
        at, off = divmod(row * COLS, LANES)
        piece = flat[:, at * LANES : (at + 1) * LANES]
        if off:
            after = flat[:, (at + 1) * LANES : (at + 2) * LANES]
            piece = jnp.where(
                lane < LANES - off,
                pltpu.roll(piece, LANES - off, 1),
                pltpu.roll(after, LANES - off, 1),
            )
        rows.append(jnp.where(lane < COLS, piece, 0.0))
    return jnp.concatenate(rows, axis=1)


def squeeze(frame):
    lane = lane_ids(OWN)
    rows = [frame[:, r * LANES : (r + 1) * LANES] for r in range(ROWS)]
    pieces = []
    for at in range(ROWS):
        row, off = divmod(at * LANES, COLS)
        piece = rows[row]
        if off:
            piece = pltpu.roll(piece, LANES - off, 1)
        if row + 1 < ROWS:
            piece = jnp.where(lane < COLS - off, piece, pltpu.roll(rows[row + 1], COLS - off, 1))
        pieces.append(piece)
    return jnp.concatenate(pieces, axis=1)[:, : ROWS * COLS]


def kernel(
    sections,
    chans,
    lat_hbm,
    w1_hbm,
    w2_hbm,
    g1_hbm,
    b1_hbm,
    g2_hbm,
    b2_hbm,
    out_ref,
    lat,
    weights,
    vecs,
    flipped,
    values,
    squares,
    partial_a,
    partial_b,
    partial_all,
    turned,
    w_out,
    w_in,
    stacked,
    sums,
    own_sums,
    shares,
    from_line,
    from_before,
    local_sem,
    all_send,
    all_recv,
    value_send,
    value_recv,
    pa_send,
    pa_recv,
    pb_send,
    pb_recv,
    w_send,
    w_recv,
    line_send,
    line_recv,
    next_send,
    next_recv,
):
    t = lax.axis_index("tm")
    chan = lax.axis_index("chan")
    x, y = lax.rem(chan, SIDE), lax.div(chan, SIDE)
    parity = lax.rem(t, 2)

    swap = [parity, 1 - parity]
    index_a = [x + s * (y - x) for s in swap]
    index_b = [y + s * (x - y) for s in swap]

    def chan_at(j, a, b):
        s = swap[j]
        return a * (1 + (SIDE - 1) * s) + b * (SIDE - (SIDE - 1) * s)

    def shifted(index, d):
        return lax.rem(index + d, SIDE)

    def a_peer(j, d):
        return (t, chan_at(j, shifted(index_a[j], d), index_b[j]))

    def b_peer(j, d, later=0):
        return (t + later, chan_at(j, index_a[j], shifted(index_b[j], d)))

    def remote(src, dst, send, recv, device):
        return pltpu.make_async_remote_copy(
            src_ref=src,
            dst_ref=dst,
            send_sem=send,
            recv_sem=recv,
            device_id=device,
            device_id_type=pl.DeviceIdType.MESH,
        )

    far_first = (2, 1, 3)

    loads = [
        pltpu.make_async_copy(lat_hbm, lat, local_sem.at[0]),
        pltpu.make_async_copy(w1_hbm, weights.at[0], local_sem.at[1]),
        pltpu.make_async_copy(w2_hbm, weights.at[1], local_sem.at[2]),
    ]
    for n, ref in enumerate((g1_hbm, b1_hbm, g2_hbm, b2_hbm)):
        loads.append(pltpu.make_async_copy(ref, vecs.at[n], local_sem.at[3 + n]))
    for load in loads:
        load.start()

    barrier = pltpu.get_barrier_semaphore()

    def greet(device):
        pl.semaphore_signal(barrier, inc=1, device_id=device, device_id_type=pl.DeviceIdType.MESH)

    for d in range(1, SIDE):
        greet((t, SIDE * y + shifted(x, d)))
        greet((t, SIDE * shifted(y, d) + x))

    @pl.when(t > 0)
    def _():
        greet((t - 1, chan))
        for d in range(1, SIDE):
            greet((t - 1, SIDE * y + shifted(x, d)))
            greet((t - 1, SIDE * shifted(y, d) + x))

    def own_squares(f, value):
        sums_of = jnp.sum(value * value, axis=0, keepdims=True)
        for r in range(ROWS):
            squares[ROWS * f + r : ROWS * f + r + 1, :] = sums_of[:, r * LANES : (r + 1) * LANES]

    for n in range(4):
        loads[3 + n].wait()
    flipped[...] = jnp.zeros((LANES, LANES), F32)
    for n in range(4):
        flipped[n : n + 1, 0:OWN] = vecs[n]
    columns = jnp.transpose(flipped[...])[:OWN]

    def column(n):
        return jnp.broadcast_to(columns[:, n : n + 1], (OWN, LANES))

    bias = [column(1), column(3)]
    gain = [tile4(column(0)), tile4(column(2))]

    squares[...] = jnp.zeros((16, LANES), F32)
    loads[0].wait()
    for f in range(3):
        value = spread(lat[f].astype(F32))
        values[0, 0, f] = fold(value * gain[0])
        own_squares(f, value)
    partial_a[0, 0] = squares[...].astype(BF16)

    sends = []

    def start(copy):
        copy.start()
        sends.append(copy)

    def send_squares_a(j):
        for d in far_first:
            start(
                remote(
                    partial_a.at[j, 0],
                    partial_a.at[j, SIDE - d],
                    pa_send.at[j, d],
                    pa_recv.at[j, SIDE - d],
                    b_peer(j, d),
                )
            )

    def send_values(j):
        for d in far_first:
            start(
                remote(
                    values.at[j, 0],
                    values.at[j, SIDE - d],
                    value_send.at[j, d],
                    value_recv.at[j, SIDE - d],
                    a_peer(j, d),
                )
            )

    def wait_values(j, slot):
        remote(
            values.at[j, 0], values.at[j, slot], value_send.at[j, slot], value_recv.at[j, slot], a_peer(j, slot)
        ).wait_recv()

    def send_squares_b(j):
        total = partial_a[j, 0].astype(F32)
        for d in (1, 3, 2):
            remote(
                partial_a.at[j, 0], partial_a.at[j, d], pa_send.at[j, d], pa_recv.at[j, d], b_peer(j, d)
            ).wait_recv()
            total = total + partial_a[j, d].astype(F32)
        partial_b[j, 0] = total.astype(BF16)
        for d in far_first:
            start(
                remote(
                    partial_b.at[j, 0],
                    partial_b.at[j, SIDE - d],
                    pb_send.at[j, d],
                    pb_recv.at[j, SIDE - d],
                    a_peer(j, d),
                )
            )

    def scales(j):
        total = partial_b[j, 0].astype(F32)
        for d in (1, 3, 2):
            remote(
                partial_b.at[j, 0], partial_b.at[j, d], pb_send.at[j, d], pb_recv.at[j, d], a_peer(j, d)
            ).wait_recv()
            total = total + partial_b[j, d].astype(F32)
        return lax.rsqrt(total / chans + 1e-06)

    def any_copy(di, dj):
        to = (SIDE - di) % SIDE * SIDE + (SIDE - dj) % SIDE
        return remote(
            partial_all.at[0],
            partial_all.at[to],
            all_send.at[di * SIDE + dj],
            all_recv.at[to],
            (t, SIDE * shifted(y, dj) + shifted(x, di)),
        )

    others = sorted(
        [(di, dj) for di in range(SIDE) for dj in range(SIDE) if di or dj],
        key=lambda o: -min(o[0], SIDE - o[0]) - min(o[1], SIDE - o[1]),
    )

    def send_squares_all():
        for di, dj in others:
            start(any_copy(di, dj))

    def scales_all():
        total = partial_all[0].astype(F32)
        for di, dj in others[::-1]:
            any_copy(SIDE - di if di else 0, SIDE - dj if dj else 0).wait_recv()
            total = total + partial_all[di * SIDE + dj].astype(F32)
        return lax.rsqrt(total / chans + 1e-06)

    def turn_weights(j):
        loads[1 + j].wait()
        for k in range(3):
            part = weights[j, 9 * k : 9 * k + 9].astype(F32).reshape(9 * OWN, chans)
            part = jnp.concatenate([part, jnp.zeros((DEPTH - 9 * OWN, chans), F32)], axis=0)
            flat = jnp.transpose(part)
            turned[...] = flat
            for d in range(SIDE):
                rows = []
                for e in range(SIDE):
                    block = chan_at(j, shifted(index_a[j], d), shifted(index_b[j], e))
                    rows.append(turned[pl.ds(pl.multiple_of(block * OWN, 8), OWN), :])
                rows = jnp.concatenate(rows, axis=0).astype(BF16)
                if d == 0:
                    w_in[j, 0, k] = rows
                else:
                    w_out[j, d - 1, k] = rows

    def send_weights(j):
        for d in far_first:
            start(
                remote(
                    w_out.at[j, d - 1],
                    w_in.at[j, SIDE - d],
                    w_send.at[j, d],
                    w_recv.at[j, SIDE - d],
                    a_peer(j, d),
                )
            )

    def stack_taps(slot, j, scale):
        for f in range(3):
            value = unfold(values[j, slot, f])
            row = jnp.concatenate([scale[ROWS * f + r : ROWS * f + r + 1] for r in range(ROWS)], axis=1)
            normed = value * row
            act = 0.5 * normed * (1.0 + jnp.tanh(0.5 * normed))
            act = act.astype(BF16).astype(F32)
            rows = [act[:, r * LANES : (r + 1) * LANES] for r in range(ROWS)]
            shifts = [
                [pltpu.roll(r, 1, 1) for r in rows],
                rows,
                [pltpu.roll(r, LANES - 1, 1) for r in rows],
            ]
            none = jnp.zeros((OWN, LANES), F32)
            taps = []
            for dy in range(3):
                for dx in range(3):
                    moved = [none] + shifts[dx] + [none]
                    taps.append(jnp.concatenate(moved[dy : dy + ROWS], axis=1))
            taps.append(jnp.zeros((DEPTH - 9 * OWN, WIDE), F32))
            stacked[f, slot] = jnp.concatenate(taps, axis=0).astype(BF16)

    group = SIDE * OWN

    def emit(j, frame, total):
        for e in range(SIDE):
            piece = total[e * OWN : (e + 1) * OWN]
            if e == 0 and frame < 3:
                own_sums[frame] = piece
            else:
                shares[j, e, frame] = fold(piece)

    def emit_all(j, product):
        last = product(2)
        emit(j, 4, last[:group])
        sums[2, :group] = last[group : 2 * group]
        sums[2, group : 2 * group] = last[2 * group :]
        mid = product(1)
        emit(j, 3, sums[2, :group] + mid[:group])
        sums[2, group : 2 * group] += mid[group : 2 * group]
        sums[2, :group] = mid[2 * group :]

        @pl.when(t < sections - 1)
        def _():
            for e in range(SIDE):
                next_copy(j, e).start()

        first = product(0)
        emit(j, 2, sums[2, group : 2 * group] + first[:group])
        emit(j, 1, sums[2, :group] + first[group : 2 * group])
        emit(j, 0, first[2 * group :])
        for d in far_first:
            start(line_copy(j, d))

    def left_of(j, slot):
        return w_in[j, slot].reshape(3 * group, DEPTH)

    def wait_weights(j, slot):
        remote(
            w_out.at[j, 0], w_in.at[j, slot], w_send.at[j, slot], w_recv.at[j, slot], a_peer(j, slot)
        ).wait_recv()

    def convolve_as_weights_come(j):
        for slot in (0, 1, 3):
            if slot:
                wait_weights(j, slot)
            for f in range(3):
                part = jnp.dot(left_of(j, slot), stacked[f, slot], preferred_element_type=F32)
                if slot:
                    part = part + sums[f]
                sums[f] = part
        wait_weights(j, 2)
        emit_all(j, lambda f: sums[f] + jnp.dot(left_of(j, 2), stacked[f, 2], preferred_element_type=F32))

    def convolve(j):
        for slot in (1, 3, 2):
            wait_weights(j, slot)
        left = jnp.concatenate([left_of(j, s) for s in range(SIDE)], axis=1)
        emit_all(
            j, lambda f: jnp.dot(left, stacked[f].reshape(SIDE * DEPTH, WIDE), preferred_element_type=F32)
        )

    def next_copy(j, e):
        return remote(
            shares.at[j, e, pl.ds(3, 2)],
            from_before.at[j, e],
            next_send.at[j, e],
            next_recv.at[j, e],
            b_peer(j, e, 1),
        )

    def line_copy(j, d):
        return remote(
            shares.at[j, d, pl.ds(0, 3)],
            from_line.at[j, SIDE - d],
            line_send.at[j, d],
            line_recv.at[j, SIDE - d],
            b_peer(j, d),
        )

    def collect(j):
        @pl.when(t > 0)
        def _():
            for e in range(SIDE):
                remote(
                    from_before.at[j, e],
                    from_before.at[j, e],
                    next_send.at[j, e],
                    next_recv.at[j, e],
                    (t, chan_at(j, shifted(index_a[j], 1), index_b[j])),
                ).wait_recv()

        for d in (1, 3, 2):
            remote(
                from_line.at[j, d],
                from_line.at[j, d],
                line_send.at[j, d],
                line_recv.at[j, d],
                b_peer(j, d),
            ).wait_recv()
        frames = []
        for f in range(3):
            total = own_sums[f] + tile4(bias[j])
            for d in range(1, SIDE):
                total = total + unfold(from_line[j, d, f])
            if f < 2:
                for e in range(SIDE):
                    total = total + unfold(from_before[j, e, f])
            frames.append(total)
        return frames

    @pl.when(t == 0)
    def _():
        from_before[...] = jnp.zeros(from_before.shape, BF16)

    turn_weights(0)
    pl.semaphore_wait(barrier, 2 * (SIDE - 1) + jnp.where(t < sections - 1, 2 * SIDE - 1, 0))
    send_squares_a(0)
    send_values(0)
    send_weights(0)
    send_squares_b(0)
    turn_weights(1)
    scale = scales(0)
    for slot in (0, 1, 3, 2):
        if slot:
            wait_values(0, slot)
        stack_taps(slot, 0, scale)
    convolve_as_weights_come(0)
    send_weights(1)

    frames = collect(0)
    keep = tile4(lane_ids(OWN)) < COLS
    for f in range(3):
        middle = jnp.where(keep, frames[f], 0.0).astype(BF16).astype(F32)
        values[1, 0, f] = fold(middle * gain[1])
        own_squares(f, middle)
    partial_all[0] = squares[...].astype(BF16)
    send_squares_all()
    send_values(1)
    scale = scales_all()
    for slot in (0, 1, 3, 2):
        if slot:
            wait_values(1, slot)
        stack_taps(slot, 1, scale)
    convolve(1)
    frames = collect(1)
    for f in range(3):
        out_ref[f] = (lat[f].astype(F32) + squeeze(frames[f])).astype(BF16)

    for copy in sends:
        copy.wait_send()

    @pl.when(t < sections - 1)
    def _():
        for j in range(2):
            for e in range(SIDE):
                next_copy(j, e).wait_send()


def block(sections, latent, gain_one, weight_one, bias_one, gain_two, weight_two, bias_two):
    frames = latent.shape[1]
    chans = weight_one.shape[3]
    dma = pltpu.SemaphoreType.DMA
    anywhere = pl.BlockSpec(memory_space=pltpu.HBM)
    result = pl.pallas_call(
        functools.partial(kernel, sections, chans),
        out_shape=jax.ShapeDtypeStruct((frames, OWN, ROWS * COLS), BF16),
        in_specs=[anywhere] * 7,
        out_specs=pl.BlockSpec(memory_space=pltpu.VMEM),
        scratch_shapes=[
            pltpu.VMEM((frames, OWN, ROWS * COLS), BF16),
            pltpu.VMEM((2, 27, OWN, chans), BF16),
            pltpu.VMEM((4, 1, OWN), F32),
            pltpu.VMEM((LANES, LANES), F32),
            pltpu.VMEM((2, SIDE, frames, 2 * OWN, HALF), BF16),
            pltpu.VMEM((16, LANES), F32),
            pltpu.VMEM((1, SIDE, 16, LANES), BF16),
            pltpu.VMEM((1, SIDE, 16, LANES), BF16),
            pltpu.VMEM((SIDE * SIDE, 16, LANES), BF16),
            pltpu.VMEM((chans, DEPTH), F32),
            pltpu.VMEM((2, SIDE - 1, 3, SIDE * OWN, DEPTH), BF16),
            pltpu.VMEM((2, SIDE, 3, SIDE * OWN, DEPTH), BF16),
            pltpu.VMEM((frames, SIDE, DEPTH, WIDE), BF16),
            pltpu.VMEM((frames, 3 * SIDE * OWN, WIDE), F32),
            pltpu.VMEM((frames, OWN, WIDE), F32),
            pltpu.VMEM((2, SIDE, frames + 2, 2 * OWN, HALF), BF16),
            pltpu.VMEM((2, SIDE, frames, 2 * OWN, HALF), BF16),
            pltpu.VMEM((2, SIDE, 2, 2 * OWN, HALF), BF16),
            dma((7,)),
            dma((SIDE * SIDE,)),
            dma((SIDE * SIDE,)),
        ]
        + [dma((2, SIDE))] * 12,
        compiler_params=pltpu.CompilerParams(
            collective_id=0, has_side_effects=True, vmem_limit_bytes=60 * 1024 * 1024
        ),
    )(
        jnp.transpose(latent, (1, 0, 2)),
        weight_one.reshape(27, OWN, chans),
        weight_two.reshape(27, OWN, chans),
        gain_one.reshape(1, OWN),
        bias_one.reshape(1, OWN),
        gain_two.reshape(1, OWN),
        bias_two.reshape(1, OWN),
    )
    return jnp.transpose(result, (1, 0, 2))


def solution(mesh):
    in_specs = (
        P("chan", "tm", None),
        P("chan"),
        P(None, None, "chan", None),
        P("chan"),
        P("chan"),
        P(None, None, "chan", None),
        P("chan"),
    )
    return jax.shard_map(
        functools.partial(block, mesh.shape["tm"]),
        mesh=mesh,
        in_specs=in_specs,
        out_specs=P("chan", "tm", None),
        check_vma=False,
    )
```

```python
import functools

import jax
import jax.numpy as jnp
from jax import lax
from jax.experimental import pallas as pl
from jax.experimental.pallas import tpu as pltpu
from jax.sharding import PartitionSpec as P

COLS = 104
ROWS = 4
LANES = 128
WIDE = ROWS * LANES
SIDE = 4
OWN = 24
HALF = WIDE // 2
DEPTH = 256
F32 = jnp.float32
BF16 = jnp.bfloat16


def unfold(value):
    value = value.astype(F32)
    return jnp.concatenate([value[:OWN], value[OWN:]], axis=1)


def fold(value):
    return jnp.concatenate([value[:, :HALF], value[:, HALF:]], axis=0).astype(BF16)


def tile4(value):
    return jnp.concatenate([value] * ROWS, axis=1)


def lane_ids(rows):
    return lax.broadcasted_iota(jnp.int32, (rows, LANES), 1)


def spread(frame):
    flat = jnp.concatenate([frame, jnp.zeros((OWN, WIDE - ROWS * COLS), F32)], axis=1)
    lane = lane_ids(OWN)
    rows = []
    for row in range(ROWS):
        at, off = divmod(row * COLS, LANES)
        piece = flat[:, at * LANES : (at + 1) * LANES]
        if off:
            after = flat[:, (at + 1) * LANES : (at + 2) * LANES]
            piece = jnp.where(
                lane < LANES - off,
                pltpu.roll(piece, LANES - off, 1),
                pltpu.roll(after, LANES - off, 1),
            )
        rows.append(jnp.where(lane < COLS, piece, 0.0))
    return jnp.concatenate(rows, axis=1)


def squeeze(frame):
    lane = lane_ids(OWN)
    rows = [frame[:, r * LANES : (r + 1) * LANES] for r in range(ROWS)]
    pieces = []
    for at in range(ROWS):
        row, off = divmod(at * LANES, COLS)
        piece = rows[row]
        if off:
            piece = pltpu.roll(piece, LANES - off, 1)
        if row + 1 < ROWS:
            piece = jnp.where(lane < COLS - off, piece, pltpu.roll(rows[row + 1], COLS - off, 1))
        pieces.append(piece)
    return jnp.concatenate(pieces, axis=1)[:, : ROWS * COLS]


def kernel(
    sections,
    chans,
    lat_hbm,
    w1_hbm,
    w2_hbm,
    g1_hbm,
    b1_hbm,
    g2_hbm,
    b2_hbm,
    out_ref,
    lat,
    weights,
    vecs,
    flipped,
    values,
    squares,
    partial_all,
    turned,
    w_out,
    w_in,
    stacked,
    sums,
    own_sums,
    shares,
    from_line,
    from_before,
    local_sem,
    all_send,
    all_recv,
    value_send,
    value_recv,
    w_send,
    w_recv,
    line_send,
    line_recv,
    next_send,
    next_recv,
    next_ready,
    ready,
):
    t = lax.axis_index("tm")
    chan = lax.axis_index("chan")
    x, y = lax.rem(chan, SIDE), lax.div(chan, SIDE)
    parity = lax.rem(t, 2)

    swap = [parity, 1 - parity]
    index_a = [x + s * (y - x) for s in swap]
    index_b = [y + s * (x - y) for s in swap]

    def chan_at(j, a, b):
        s = swap[j]
        return a * (1 + (SIDE - 1) * s) + b * (SIDE - (SIDE - 1) * s)

    def shifted(index, d):
        return lax.rem(index + d, SIDE)

    def a_peer(j, d):
        return (t, chan_at(j, shifted(index_a[j], d), index_b[j]))

    def b_peer(j, d, later=0):
        return (t + later, chan_at(j, index_a[j], shifted(index_b[j], d)))

    def remote(src, dst, send, recv, device):
        return pltpu.make_async_remote_copy(
            src_ref=src,
            dst_ref=dst,
            send_sem=send,
            recv_sem=recv,
            device_id=device,
            device_id_type=pl.DeviceIdType.MESH,
        )

    near, far, far_first = (1, 3), (2,), (2, 1, 3)

    loads = [
        pltpu.make_async_copy(lat_hbm, lat, local_sem.at[0]),
        pltpu.make_async_copy(w1_hbm, weights.at[0], local_sem.at[1]),
        pltpu.make_async_copy(w2_hbm, weights.at[1], local_sem.at[2]),
    ]
    for n, ref in enumerate((g1_hbm, b1_hbm, g2_hbm, b2_hbm)):
        loads.append(pltpu.make_async_copy(ref, vecs.at[n], local_sem.at[3 + n]))
    for load in loads:
        load.start()

    barrier = pltpu.get_barrier_semaphore()

    def tell(semaphore, device):
        pl.semaphore_signal(semaphore, inc=1, device_id=device, device_id_type=pl.DeviceIdType.MESH)

    def greet(device):
        tell(barrier, device)

    for d in (1, 2, 3):
        greet((t, SIDE * y + shifted(x, d)))
        greet((t, SIDE * shifted(y, d) + x))

    @pl.when(t < sections - 1)
    def _():
        greet((t + 1, chan))

    def own_squares(f, value):
        sums_of = jnp.sum(value * value, axis=0, keepdims=True)
        for r in range(ROWS):
            squares[ROWS * f + r : ROWS * f + r + 1, :] = sums_of[:, r * LANES : (r + 1) * LANES]

    for n in range(4):
        loads[3 + n].wait()
    flipped[...] = jnp.zeros((LANES, LANES), F32)
    for n in range(4):
        flipped[n : n + 1, 0:OWN] = vecs[n]
    columns = jnp.transpose(flipped[...])[:OWN]

    def column(n):
        return jnp.broadcast_to(columns[:, n : n + 1], (OWN, LANES))

    bias = [column(1), column(3)]
    gain = [tile4(column(0)), tile4(column(2))]

    squares[...] = jnp.zeros((16, LANES), F32)
    loads[0].wait()
    for f in range(3):
        value = spread(lat[f].astype(F32))
        values[0, 0, f] = fold(value * gain[0])
        own_squares(f, value)
    partial_all[0, 0] = squares[...].astype(BF16)

    sends = []

    def start(copy):
        copy.start()
        sends.append(copy)

    def send_values(j, steps):
        for d in steps:
            start(
                remote(
                    values.at[j, 0],
                    values.at[j, SIDE - d],
                    value_send.at[j, d],
                    value_recv.at[j, SIDE - d],
                    a_peer(j, d),
                )
            )

    def wait_values(j, slot):
        remote(
            values.at[j, 0], values.at[j, slot], value_send.at[j, slot], value_recv.at[j, slot], a_peer(j, slot)
        ).wait_recv()

    def any_copy(j, di, dj):
        to = (SIDE - di) % SIDE * SIDE + (SIDE - dj) % SIDE
        return remote(
            partial_all.at[j, 0],
            partial_all.at[j, to],
            all_send.at[j, di * SIDE + dj],
            all_recv.at[j, to],
            (t, SIDE * shifted(y, dj) + shifted(x, di)),
        )

    others = sorted(
        [(di, dj) for di in range(SIDE) for dj in range(SIDE) if di or dj],
        key=lambda o: -min(o[0], SIDE - o[0]) - min(o[1], SIDE - o[1]),
    )

    def send_squares_all(j):
        for di, dj in others:
            start(any_copy(j, di, dj))

    def scales_all(j):
        total = partial_all[j, 0].astype(F32)
        for di, dj in others[::-1]:
            any_copy(j, SIDE - di if di else 0, SIDE - dj if dj else 0).wait_recv()
            total = total + partial_all[j, di * SIDE + dj].astype(F32)
        return lax.rsqrt(total / chans + 1e-06)

    def turn_weights(j):
        loads[1 + j].wait()
        for k in range(3):
            part = weights[j, 9 * k : 9 * k + 9].astype(F32).reshape(9 * OWN, chans)
            part = jnp.concatenate([part, jnp.zeros((DEPTH - 9 * OWN, chans), F32)], axis=0)
            flat = jnp.transpose(part)
            turned[...] = flat
            for d in range(SIDE):
                rows = []
                for e in range(SIDE):
                    block = chan_at(j, shifted(index_a[j], d), shifted(index_b[j], e))
                    rows.append(turned[pl.ds(pl.multiple_of(block * OWN, 8), OWN), :])
                rows = jnp.concatenate(rows, axis=0).astype(BF16)
                if d == 0:
                    w_in[j, 0, k] = rows
                else:
                    w_out[j, d - 1, k] = rows

    def send_weights(j, steps):
        for d in steps:
            start(
                remote(
                    w_out.at[j, d - 1],
                    w_in.at[j, SIDE - d],
                    w_send.at[j, d],
                    w_recv.at[j, SIDE - d],
                    a_peer(j, d),
                )
            )

    def stack_taps(slot, j, scale):
        for f in range(3):
            value = unfold(values[j, slot, f])
            row = jnp.concatenate([scale[ROWS * f + r : ROWS * f + r + 1] for r in range(ROWS)], axis=1)
            normed = value * row
            act = 0.5 * normed * (1.0 + jnp.tanh(0.5 * normed))
            act = act.astype(BF16).astype(F32)
            rows = [act[:, r * LANES : (r + 1) * LANES] for r in range(ROWS)]
            shifts = [
                [pltpu.roll(r, 1, 1) for r in rows],
                rows,
                [pltpu.roll(r, LANES - 1, 1) for r in rows],
            ]
            none = jnp.zeros((OWN, LANES), F32)
            taps = []
            for dy in range(3):
                for dx in range(3):
                    moved = [none] + shifts[dx] + [none]
                    taps.append(jnp.concatenate(moved[dy : dy + ROWS], axis=1))
            taps.append(jnp.zeros((DEPTH - 9 * OWN, WIDE), F32))
            stacked[f, slot] = jnp.concatenate(taps, axis=0).astype(BF16)

    group = SIDE * OWN

    def emit(j, frame, total):
        for e in range(SIDE):
            piece = total[e * OWN : (e + 1) * OWN]
            if e == 0 and frame < 3:
                own_sums[frame] = piece
            else:
                shares[j, e, frame] = fold(piece)

    def emit_all(j, product):
        last = product(2)
        emit(j, 4, last[:group])
        sums[2, :group] = last[group : 2 * group]
        sums[2, group : 2 * group] = last[2 * group :]
        mid = product(1)
        emit(j, 3, sums[2, :group] + mid[:group])
        sums[2, group : 2 * group] += mid[group : 2 * group]
        sums[2, :group] = mid[2 * group :]

        @pl.when(t < sections - 1)
        def _():
            if j == 0:
                pl.semaphore_wait(next_ready, 1)
            for e in range(SIDE):
                next_copy(j, e).start()

        first = product(0)
        emit(j, 2, sums[2, group : 2 * group] + first[:group])
        emit(j, 1, sums[2, :group] + first[group : 2 * group])
        emit(j, 0, first[2 * group :])
        for d in far_first:
            start(line_copy(j, d))

    def left_of(j, slot):
        return w_in[j, slot].reshape(3 * group, DEPTH)

    def wait_weights(j, slot):
        remote(
            w_out.at[j, 0], w_in.at[j, slot], w_send.at[j, slot], w_recv.at[j, slot], a_peer(j, slot)
        ).wait_recv()

    def convolve_as_weights_come(j):
        for slot in (0, 1, 3):
            if slot:
                wait_weights(j, slot)
            for f in range(3):
                part = jnp.dot(left_of(j, slot), stacked[f, slot], preferred_element_type=F32)
                if slot:
                    part = part + sums[f]
                sums[f] = part
        wait_weights(j, 2)
        emit_all(j, lambda f: sums[f] + jnp.dot(left_of(j, 2), stacked[f, 2], preferred_element_type=F32))

    def convolve(j):
        for slot in (1, 3, 2):
            wait_weights(j, slot)
        left = jnp.concatenate([left_of(j, s) for s in range(SIDE)], axis=1)
        emit_all(
            j, lambda f: jnp.dot(left, stacked[f].reshape(SIDE * DEPTH, WIDE), preferred_element_type=F32)
        )

    def next_copy(j, e):
        return remote(
            shares.at[j, e, pl.ds(3, 2)],
            from_before.at[j, e],
            next_send.at[j, e],
            next_recv.at[j, e],
            b_peer(j, e, 1),
        )

    def line_copy(j, d):
        return remote(
            shares.at[j, d, pl.ds(0, 3)],
            from_line.at[j, SIDE - d],
            line_send.at[j, d],
            line_recv.at[j, SIDE - d],
            b_peer(j, d),
        )

    def collect(j):
        @pl.when(t > 0)
        def _():
            for e in range(SIDE):
                remote(
                    from_before.at[j, e],
                    from_before.at[j, e],
                    next_send.at[j, e],
                    next_recv.at[j, e],
                    (t, chan_at(j, shifted(index_a[j], 1), index_b[j])),
                ).wait_recv()

        for d in (1, 3, 2):
            remote(
                from_line.at[j, d],
                from_line.at[j, d],
                line_send.at[j, d],
                line_recv.at[j, d],
                b_peer(j, d),
            ).wait_recv()
        frames = []
        for f in range(3):
            total = own_sums[f] + tile4(bias[j])
            for d in range(1, SIDE):
                total = total + unfold(from_line[j, d, f])
            if f < 2:
                for e in range(SIDE):
                    total = total + unfold(from_before[j, e, f])
            frames.append(total)
        return frames

    @pl.when(t == 0)
    def _():
        from_before[...] = jnp.zeros(from_before.shape, BF16)

    turn_weights(0)
    pl.semaphore_wait(barrier, 6 + jnp.where(t > 0, 1, 0))
    for d in (1, 2, 3):
        tell(ready, (t, SIDE * y + shifted(x, d)))
    send_weights(0, near)
    pl.semaphore_wait(ready, 3)
    send_squares_all(0)
    send_values(0, far_first)
    send_weights(0, far)

    @pl.when(t > 0)
    def _():
        tell(next_ready, (t - 1, chan))

    turn_weights(1)
    scale = scales_all(0)
    for slot in (0, 1, 3, 2):
        if slot:
            wait_values(0, slot)
        stack_taps(slot, 0, scale)
    convolve_as_weights_come(0)
    send_weights(1, far_first)

    frames = collect(0)
    keep = tile4(lane_ids(OWN)) < COLS
    for f in range(3):
        middle = jnp.where(keep, frames[f], 0.0).astype(BF16).astype(F32)
        values[1, 0, f] = fold(middle * gain[1])
        own_squares(f, middle)
    partial_all[1, 0] = squares[...].astype(BF16)
    send_squares_all(1)
    send_values(1, far_first)
    scale = scales_all(1)
    for slot in (0, 1, 3, 2):
        if slot:
            wait_values(1, slot)
        stack_taps(slot, 1, scale)
    convolve(1)
    frames = collect(1)
    for f in range(3):
        out_ref[f] = (lat[f].astype(F32) + squeeze(frames[f])).astype(BF16)

    for copy in sends:
        copy.wait_send()

    @pl.when(t < sections - 1)
    def _():
        for j in range(2):
            for e in range(SIDE):
                next_copy(j, e).wait_send()


def block(sections, latent, gain_one, weight_one, bias_one, gain_two, weight_two, bias_two):
    frames = latent.shape[1]
    chans = weight_one.shape[3]
    dma = pltpu.SemaphoreType.DMA
    anywhere = pl.BlockSpec(memory_space=pltpu.HBM)
    result = pl.pallas_call(
        functools.partial(kernel, sections, chans),
        out_shape=jax.ShapeDtypeStruct((frames, OWN, ROWS * COLS), BF16),
        in_specs=[anywhere] * 7,
        out_specs=pl.BlockSpec(memory_space=pltpu.VMEM),
        scratch_shapes=[
            pltpu.VMEM((frames, OWN, ROWS * COLS), BF16),
            pltpu.VMEM((2, 27, OWN, chans), BF16),
            pltpu.VMEM((4, 1, OWN), F32),
            pltpu.VMEM((LANES, LANES), F32),
            pltpu.VMEM((2, SIDE, frames, 2 * OWN, HALF), BF16),
            pltpu.VMEM((16, LANES), F32),
            pltpu.VMEM((2, SIDE * SIDE, 16, LANES), BF16),
            pltpu.VMEM((chans, DEPTH), F32),
            pltpu.VMEM((2, SIDE - 1, 3, SIDE * OWN, DEPTH), BF16),
            pltpu.VMEM((2, SIDE, 3, SIDE * OWN, DEPTH), BF16),
            pltpu.VMEM((frames, SIDE, DEPTH, WIDE), BF16),
            pltpu.VMEM((frames, 3 * SIDE * OWN, WIDE), F32),
            pltpu.VMEM((frames, OWN, WIDE), F32),
            pltpu.VMEM((2, SIDE, frames + 2, 2 * OWN, HALF), BF16),
            pltpu.VMEM((2, SIDE, frames, 2 * OWN, HALF), BF16),
            pltpu.VMEM((2, SIDE, 2, 2 * OWN, HALF), BF16),
            dma((7,)),
            dma((2, SIDE * SIDE)),
            dma((2, SIDE * SIDE)),
        ]
        + [dma((2, SIDE))] * 8
        + [pltpu.SemaphoreType.REGULAR] * 2,
        compiler_params=pltpu.CompilerParams(
            collective_id=0, has_side_effects=True, vmem_limit_bytes=40 * 1024 * 1024
        ),
    )(
        *[pltpu.with_memory_space_constraint(v, pltpu.HBM) for v in (
        jnp.transpose(latent, (1, 0, 2)),
        weight_one.reshape(27, OWN, chans),
        weight_two.reshape(27, OWN, chans),
        gain_one.reshape(1, OWN),
        bias_one.reshape(1, OWN),
        gain_two.reshape(1, OWN),
        bias_two.reshape(1, OWN),
    )]
    )
    return jnp.transpose(result, (1, 0, 2))


def solution(mesh):
    in_specs = (
        P("chan", "tm", None),
        P("chan"),
        P(None, None, "chan", None),
        P("chan"),
        P("chan"),
        P(None, None, "chan", None),
        P("chan"),
    )
    return jax.shard_map(
        functools.partial(block, mesh.shape["tm"]),
        mesh=mesh,
        in_specs=in_specs,
        out_specs=P("chan", "tm", None),
        check_vma=False,
    )
```

```python
import functools

import jax
import jax.numpy as jnp
from jax import lax
from jax.experimental import pallas as pl
from jax.experimental.pallas import tpu as pltpu
from jax.sharding import PartitionSpec as P

COLS = 104
ROWS = 4
LANES = 128
WIDE = ROWS * LANES
SIDE = 4
OWN = 24
FRAMES = 3
MAIN = 384
REST = ROWS * COLS - MAIN
PACKED = FRAMES * MAIN + LANES
PACKED_NEXT = 2 * MAIN + LANES
DEPTH = 256
F32 = jnp.float32
BF16 = jnp.bfloat16


def unfold(value):
    value = value.astype(F32)
    return jnp.concatenate([value[:OWN], value[OWN:]], axis=1)


def fold(value):
    half = PACKED // 2
    return jnp.concatenate([value[:, :half], value[:, half:]], axis=0).astype(BF16)


NEXT_HALF = (OWN // 8 * PACKED_NEXT + LANES) // 2


def fold_next(value):
    parts = [value[8 * n : 8 * n + 8] for n in range(OWN // 8)] + [jnp.zeros((8, LANES), F32)]
    flat = jnp.concatenate(parts, axis=1)
    return jnp.concatenate([flat[:, :NEXT_HALF], flat[:, NEXT_HALF:]], axis=0).astype(BF16)


def unfold_next(value):
    value = value.astype(F32)
    flat = jnp.concatenate([value[:8], value[8:]], axis=1)
    return jnp.concatenate(
        [flat[:, PACKED_NEXT * n : PACKED_NEXT * (n + 1)] for n in range(OWN // 8)], axis=0
    )


def spread_lanes(value):
    return jnp.concatenate([value] * (PACKED // LANES), axis=1)


def lane_ids(rows):
    return lax.broadcasted_iota(jnp.int32, (rows, LANES), 1)


def tiles(value):
    return [value[:, n : n + LANES] for n in range(0, value.shape[1], LANES)]


def spread(packed, f):
    parts = tiles(packed)
    cells = parts[3 * f : 3 * f + 3] + [pltpu.roll(parts[-1], LANES - REST * f, 1) if f else parts[-1]]
    lane = lane_ids(OWN)
    rows = []
    for row in range(ROWS):
        at, off = divmod(row * COLS, LANES)
        piece = cells[at]
        if off:
            piece = jnp.where(
                lane < LANES - off,
                pltpu.roll(piece, LANES - off, 1),
                pltpu.roll(cells[at + 1], LANES - off, 1),
            )
        rows.append(jnp.where(lane < COLS, piece, 0.0))
    return rows


def pack(frame, place):
    rows = tiles(frame)
    lane = lane_ids(frame.shape[0])
    pieces = []
    for at in range(MAIN // LANES):
        row, off = divmod(at * LANES, COLS)
        piece = pltpu.roll(rows[row], LANES - off, 1) if off else rows[row]
        pieces.append(jnp.where(lane < COLS - off, piece, pltpu.roll(rows[row + 1], COLS - off, 1)))
    row, off = divmod(MAIN, COLS)
    return jnp.concatenate(pieces, axis=1), pltpu.roll(rows[row], (LANES - off + REST * place) % LANES, 1)


def join(packs):
    lane = lane_ids(packs[0][0].shape[0])
    rest = jnp.zeros(packs[0][1].shape, F32)
    for place in range(len(packs) - 1, -1, -1):
        rest = jnp.where(lane < REST * (place + 1), packs[place][1], rest)
    return jnp.concatenate([main for main, _ in packs] + [rest], axis=1)


def pack_latent(lat):
    packs = []
    for f in range(FRAMES):
        frame = lat[f].astype(F32)
        rest = jnp.concatenate([frame[:, MAIN:], jnp.zeros((OWN, LANES - REST), F32)], axis=1)
        packs.append((frame[:, :MAIN], pltpu.roll(rest, REST * f, 1) if f else rest))
    return join(packs)


def kernel(
    sections,
    chans,
    lat_hbm,
    w1_hbm,
    w2_hbm,
    g1_hbm,
    b1_hbm,
    g2_hbm,
    b2_hbm,
    out_ref,
    lat,
    weights,
    vecs,
    flipped,
    values,
    squares,
    partial_all,
    turned,
    w_out,
    w_in,
    stacked,
    sums,
    own_sums,
    shares,
    shares_next,
    from_line,
    from_before,
    local_sem,
    all_send,
    all_recv,
    value_send,
    value_recv,
    w_send,
    w_recv,
    line_send,
    line_recv,
    next_send,
    next_recv,
    next_ready,
    ready,
):
    t = lax.axis_index("tm")
    chan = lax.axis_index("chan")
    x, y = lax.rem(chan, SIDE), lax.div(chan, SIDE)
    parity = lax.rem(t, 2)

    swap = [parity, 1 - parity]
    index_a = [x + s * (y - x) for s in swap]
    index_b = [y + s * (x - y) for s in swap]

    def chan_at(j, a, b):
        s = swap[j]
        return a * (1 + (SIDE - 1) * s) + b * (SIDE - (SIDE - 1) * s)

    def shifted(index, d):
        return lax.rem(index + d, SIDE)

    def a_peer(j, d):
        return (t, chan_at(j, shifted(index_a[j], d), index_b[j]))

    def b_peer(j, d, later=0):
        return (t + later, chan_at(j, index_a[j], shifted(index_b[j], d)))

    def remote(src, dst, send, recv, device):
        return pltpu.make_async_remote_copy(
            src_ref=src,
            dst_ref=dst,
            send_sem=send,
            recv_sem=recv,
            device_id=device,
            device_id_type=pl.DeviceIdType.MESH,
        )

    near, far, far_first = (1, 3), (2,), (2, 1, 3)

    loads = [
        pltpu.make_async_copy(lat_hbm, lat, local_sem.at[0]),
        pltpu.make_async_copy(w1_hbm, weights.at[0], local_sem.at[1]),
        pltpu.make_async_copy(w2_hbm, weights.at[1], local_sem.at[2]),
    ]
    for n, ref in enumerate((g1_hbm, b1_hbm, g2_hbm, b2_hbm)):
        loads.append(pltpu.make_async_copy(ref, vecs.at[n], local_sem.at[3 + n]))
    for load in loads:
        load.start()

    barrier = pltpu.get_barrier_semaphore()

    def tell(semaphore, device):
        pl.semaphore_signal(semaphore, inc=1, device_id=device, device_id_type=pl.DeviceIdType.MESH)

    def greet(device):
        tell(barrier, device)

    for d in (1, 2, 3):
        greet((t, SIDE * y + shifted(x, d)))
        greet((t, SIDE * shifted(y, d) + x))

    @pl.when(t < sections - 1)
    def _():
        greet((t + 1, chan))

    def own_squares(value):
        sums_of = jnp.sum(value * value, axis=0, keepdims=True)
        for n, part in enumerate(tiles(sums_of)):
            squares[n : n + 1, :] = part

    for n in range(4):
        loads[3 + n].wait()
    flipped[...] = jnp.zeros((LANES, LANES), F32)
    for n in range(4):
        flipped[n : n + 1, 0:OWN] = vecs[n]
    columns = jnp.transpose(flipped[...])[:OWN]

    def column(n):
        return jnp.broadcast_to(columns[:, n : n + 1], (OWN, LANES))

    bias = [column(1), column(3)]
    gain = [spread_lanes(column(0)), spread_lanes(column(2))]

    squares[...] = jnp.zeros((16, LANES), F32)
    loads[0].wait()
    value = pack_latent(lat)
    values[0, 0] = fold(value * gain[0])
    own_squares(value)
    partial_all[0, 0] = squares[...].astype(BF16)

    sends = []

    def start(copy):
        copy.start()
        sends.append(copy)

    def send_values(j, steps):
        for d in steps:
            start(
                remote(
                    values.at[j, 0],
                    values.at[j, SIDE - d],
                    value_send.at[j, d],
                    value_recv.at[j, SIDE - d],
                    a_peer(j, d),
                )
            )

    def wait_values(j, slot):
        remote(
            values.at[j, 0], values.at[j, slot], value_send.at[j, slot], value_recv.at[j, slot], a_peer(j, slot)
        ).wait_recv()

    def any_copy(j, di, dj):
        to = (SIDE - di) % SIDE * SIDE + (SIDE - dj) % SIDE
        return remote(
            partial_all.at[j, 0],
            partial_all.at[j, to],
            all_send.at[j, di * SIDE + dj],
            all_recv.at[j, to],
            (t, SIDE * shifted(y, dj) + shifted(x, di)),
        )

    others = sorted(
        [(di, dj) for di in range(SIDE) for dj in range(SIDE) if di or dj],
        key=lambda o: -min(o[0], SIDE - o[0]) - min(o[1], SIDE - o[1]),
    )

    def send_squares_all(j):
        for di, dj in others:
            start(any_copy(j, di, dj))

    def scales_all(j):
        total = partial_all[j, 0].astype(F32)
        for di, dj in others[::-1]:
            any_copy(j, SIDE - di if di else 0, SIDE - dj if dj else 0).wait_recv()
            total = total + partial_all[j, di * SIDE + dj].astype(F32)
        return lax.rsqrt(total / chans + 1e-06)

    def turn_weights(j):
        loads[1 + j].wait()
        for k in range(3):
            part = weights[j, 9 * k : 9 * k + 9].astype(F32).reshape(9 * OWN, chans)
            part = jnp.concatenate([part, jnp.zeros((DEPTH - 9 * OWN, chans), F32)], axis=0)
            flat = jnp.transpose(part)
            turned[...] = flat
            for d in range(SIDE):
                rows = []
                for e in range(SIDE):
                    block = chan_at(j, shifted(index_a[j], d), shifted(index_b[j], e))
                    rows.append(turned[pl.ds(pl.multiple_of(block * OWN, 8), OWN), :])
                rows = jnp.concatenate(rows, axis=0).astype(BF16)
                if d == 0:
                    w_in[j, 0, k] = rows
                else:
                    w_out[j, d - 1, k] = rows

    def send_weights(j, steps):
        for d in steps:
            start(
                remote(
                    w_out.at[j, d - 1],
                    w_in.at[j, SIDE - d],
                    w_send.at[j, d],
                    w_recv.at[j, SIDE - d],
                    a_peer(j, d),
                )
            )

    def stack_taps(slot, j, scale):
        normed = unfold(values[j, slot]) * jnp.concatenate([scale[n : n + 1] for n in range(PACKED // LANES)], axis=1)
        act = 0.5 * normed * (1.0 + jnp.tanh(0.5 * normed))
        act = act.astype(BF16).astype(F32)
        for f in range(FRAMES):
            rows = spread(act, f)
            shifts = [
                [pltpu.roll(r, 1, 1) for r in rows],
                rows,
                [pltpu.roll(r, LANES - 1, 1) for r in rows],
            ]
            none = jnp.zeros((OWN, LANES), F32)
            taps = []
            for dy in range(3):
                for dx in range(3):
                    moved = [none] + shifts[dx] + [none]
                    taps.append(jnp.concatenate(moved[dy : dy + ROWS], axis=1))
            taps.append(jnp.zeros((DEPTH - 9 * OWN, WIDE), F32))
            stacked[f, slot] = jnp.concatenate(taps, axis=0).astype(BF16)

    group = SIDE * OWN

    def emit_all(j, product):
        last = product(2)
        later = pack(last[:group], 1)
        sums[2, :group] = last[group : 2 * group]
        sums[2, group : 2 * group] = last[2 * group :]
        mid = product(1)
        later = join([pack(sums[2, :group] + mid[:group], 0), later])
        for e in range(SIDE):
            shares_next[j, e] = fold_next(later[e * OWN : (e + 1) * OWN])
        sums[2, group : 2 * group] += mid[group : 2 * group]
        sums[2, :group] = mid[2 * group :]

        @pl.when(t < sections - 1)
        def _():
            if j == 0:
                pl.semaphore_wait(next_ready, 1)
            for e in range(SIDE):
                next_copy(j, e).start()

        first = product(0)
        frames = [
            first[2 * group :],
            sums[2, :group] + first[group : 2 * group],
            sums[2, group : 2 * group] + first[:group],
        ]
        packed = join([pack(frame, f) for f, frame in enumerate(frames)])
        own_sums[...] = packed[:OWN]
        for e in range(1, SIDE):
            shares[j, e] = fold(packed[e * OWN : (e + 1) * OWN])
        for d in far_first:
            start(line_copy(j, d))

    def left_of(j, slot):
        return w_in[j, slot].reshape(3 * group, DEPTH)

    def wait_weights(j, slot):
        remote(
            w_out.at[j, 0], w_in.at[j, slot], w_send.at[j, slot], w_recv.at[j, slot], a_peer(j, slot)
        ).wait_recv()

    def convolve_as_weights_come(j):
        for slot in (0, 1, 3):
            if slot:
                wait_weights(j, slot)
            for f in range(3):
                part = jnp.dot(left_of(j, slot), stacked[f, slot], preferred_element_type=F32)
                if slot:
                    part = part + sums[f]
                sums[f] = part
        wait_weights(j, 2)
        emit_all(j, lambda f: sums[f] + jnp.dot(left_of(j, 2), stacked[f, 2], preferred_element_type=F32))

    def convolve(j):
        for slot in (1, 3, 2):
            wait_weights(j, slot)
        left = jnp.concatenate([left_of(j, s) for s in range(SIDE)], axis=1)
        emit_all(
            j, lambda f: jnp.dot(left, stacked[f].reshape(SIDE * DEPTH, WIDE), preferred_element_type=F32)
        )

    def next_copy(j, e):
        return remote(
            shares_next.at[j, e],
            from_before.at[j, e],
            next_send.at[j, e],
            next_recv.at[j, e],
            b_peer(j, e, 1),
        )

    def line_copy(j, d):
        return remote(
            shares.at[j, d],
            from_line.at[j, SIDE - d],
            line_send.at[j, d],
            line_recv.at[j, SIDE - d],
            b_peer(j, d),
        )

    def collect(j):
        @pl.when(t > 0)
        def _():
            for e in range(SIDE):
                remote(
                    from_before.at[j, e],
                    from_before.at[j, e],
                    next_send.at[j, e],
                    next_recv.at[j, e],
                    (t, chan_at(j, shifted(index_a[j], 1), index_b[j])),
                ).wait_recv()

        for d in (1, 3, 2):
            remote(
                from_line.at[j, d],
                from_line.at[j, d],
                line_send.at[j, d],
                line_recv.at[j, d],
                b_peer(j, d),
            ).wait_recv()
        total = own_sums[...] + spread_lanes(bias[j])
        for d in range(1, SIDE):
            total = total + unfold(from_line[j, d])
        before = unfold_next(from_before[j, 0])
        for e in range(1, SIDE):
            before = before + unfold_next(from_before[j, e])
        return jnp.concatenate(
            [
                total[:, : 2 * MAIN] + before[:, : 2 * MAIN],
                total[:, 2 * MAIN : 3 * MAIN],
                total[:, 3 * MAIN :] + before[:, 2 * MAIN :],
            ],
            axis=1,
        )

    @pl.when(t == 0)
    def _():
        from_before[...] = jnp.zeros(from_before.shape, BF16)

    turn_weights(0)
    pl.semaphore_wait(barrier, 6 + jnp.where(t > 0, 1, 0))
    for d in (1, 2, 3):
        tell(ready, (t, SIDE * y + shifted(x, d)))
    send_weights(0, near)
    pl.semaphore_wait(ready, 3)
    send_squares_all(0)
    send_values(0, far_first)
    send_weights(0, far)

    @pl.when(t > 0)
    def _():
        tell(next_ready, (t - 1, chan))

    turn_weights(1)
    scale = scales_all(0)
    for slot in (0, 1, 3, 2):
        if slot:
            wait_values(0, slot)
        stack_taps(slot, 0, scale)
    convolve_as_weights_come(0)
    send_weights(1, far_first)

    middle = collect(0)
    rest = jnp.where(lane_ids(OWN) < FRAMES * REST, middle[:, FRAMES * MAIN :], 0.0)
    middle = jnp.concatenate([middle[:, : FRAMES * MAIN], rest], axis=1).astype(BF16).astype(F32)
    values[1, 0] = fold(middle * gain[1])
    own_squares(middle)
    partial_all[1, 0] = squares[...].astype(BF16)
    send_squares_all(1)
    send_values(1, far_first)
    scale = scales_all(1)
    for slot in (0, 1, 3, 2):
        if slot:
            wait_values(1, slot)
        stack_taps(slot, 1, scale)
    convolve(1)
    result = pack_latent(lat) + collect(1)
    for f in range(FRAMES):
        rest = result[:, FRAMES * MAIN :]
        rest = pltpu.roll(rest, LANES - REST * f, 1) if f else rest
        frame = jnp.concatenate([result[:, f * MAIN : (f + 1) * MAIN], rest], axis=1)
        out_ref[f] = frame[:, : ROWS * COLS].astype(BF16)

    for copy in sends:
        copy.wait_send()

    @pl.when(t < sections - 1)
    def _():
        for j in range(2):
            for e in range(SIDE):
                next_copy(j, e).wait_send()


def block(sections, latent, gain_one, weight_one, bias_one, gain_two, weight_two, bias_two):
    frames = latent.shape[1]
    chans = weight_one.shape[3]
    dma = pltpu.SemaphoreType.DMA
    anywhere = pl.BlockSpec(memory_space=pltpu.HBM)
    result = pl.pallas_call(
        functools.partial(kernel, sections, chans),
        out_shape=jax.ShapeDtypeStruct((frames, OWN, ROWS * COLS), BF16),
        in_specs=[anywhere] * 7,
        out_specs=pl.BlockSpec(memory_space=pltpu.VMEM),
        scratch_shapes=[
            pltpu.VMEM((frames, OWN, ROWS * COLS), BF16),
            pltpu.VMEM((2, 27, OWN, chans), BF16),
            pltpu.VMEM((4, 1, OWN), F32),
            pltpu.VMEM((LANES, LANES), F32),
            pltpu.VMEM((2, SIDE, 2 * OWN, PACKED // 2), BF16),
            pltpu.VMEM((16, LANES), F32),
            pltpu.VMEM((2, SIDE * SIDE, 16, LANES), BF16),
            pltpu.VMEM((chans, DEPTH), F32),
            pltpu.VMEM((2, SIDE - 1, 3, SIDE * OWN, DEPTH), BF16),
            pltpu.VMEM((2, SIDE, 3, SIDE * OWN, DEPTH), BF16),
            pltpu.VMEM((frames, SIDE, DEPTH, WIDE), BF16),
            pltpu.VMEM((frames, 3 * SIDE * OWN, WIDE), F32),
            pltpu.VMEM((OWN, PACKED), F32),
            pltpu.VMEM((2, SIDE, 2 * OWN, PACKED // 2), BF16),
            pltpu.VMEM((2, SIDE, 16, NEXT_HALF), BF16),
            pltpu.VMEM((2, SIDE, 2 * OWN, PACKED // 2), BF16),
            pltpu.VMEM((2, SIDE, 16, NEXT_HALF), BF16),
            dma((7,)),
            dma((2, SIDE * SIDE)),
            dma((2, SIDE * SIDE)),
        ]
        + [dma((2, SIDE))] * 8
        + [pltpu.SemaphoreType.REGULAR] * 2,
        compiler_params=pltpu.CompilerParams(
            collective_id=0, has_side_effects=True, vmem_limit_bytes=40 * 1024 * 1024
        ),
    )(
        *[pltpu.with_memory_space_constraint(v, pltpu.HBM) for v in (
        jnp.transpose(latent, (1, 0, 2)),
        weight_one.reshape(27, OWN, chans),
        weight_two.reshape(27, OWN, chans),
        gain_one.reshape(1, OWN),
        bias_one.reshape(1, OWN),
        gain_two.reshape(1, OWN),
        bias_two.reshape(1, OWN),
    )]
    )
    return jnp.transpose(result, (1, 0, 2))


def solution(mesh):
    in_specs = (
        P("chan", "tm", None),
        P("chan"),
        P(None, None, "chan", None),
        P("chan"),
        P("chan"),
        P(None, None, "chan", None),
        P("chan"),
    )
    return jax.shard_map(
        functools.partial(block, mesh.shape["tm"]),
        mesh=mesh,
        in_specs=in_specs,
        out_specs=P("chan", "tm", None),
        check_vma=False,
    )
```

```python
import functools

import jax
import jax.numpy as jnp
from jax import lax
from jax.experimental import pallas as pl
from jax.experimental.pallas import tpu as pltpu
from jax.sharding import PartitionSpec as P

COLS = 104
ROWS = 4
LANES = 128
WIDE = ROWS * LANES
SIDE = 4
OWN = 24
FRAMES = 3
MAIN = 384
REST = ROWS * COLS - MAIN
PACKED = FRAMES * MAIN + LANES
PACKED_NEXT = 2 * MAIN + LANES
DEPTH = 256
F32 = jnp.float32
BF16 = jnp.bfloat16


def unfold(value):
    value = value.astype(F32)
    return jnp.concatenate([value[:OWN], value[OWN:]], axis=1)


def fold(value):
    half = PACKED // 2
    return jnp.concatenate([value[:, :half], value[:, half:]], axis=0).astype(BF16)


NEXT_HALF = (OWN // 8 * PACKED_NEXT + LANES) // 2


def fold_next(value):
    parts = [value[8 * n : 8 * n + 8] for n in range(OWN // 8)] + [jnp.zeros((8, LANES), F32)]
    flat = jnp.concatenate(parts, axis=1)
    return jnp.concatenate([flat[:, :NEXT_HALF], flat[:, NEXT_HALF:]], axis=0).astype(BF16)


def unfold_next(value):
    value = value.astype(F32)
    flat = jnp.concatenate([value[:8], value[8:]], axis=1)
    return jnp.concatenate(
        [flat[:, PACKED_NEXT * n : PACKED_NEXT * (n + 1)] for n in range(OWN // 8)], axis=0
    )


def spread_lanes(value):
    return jnp.concatenate([value] * (PACKED // LANES), axis=1)


def lane_ids(rows):
    return lax.broadcasted_iota(jnp.int32, (rows, LANES), 1)


def tiles(value):
    return [value[:, n : n + LANES] for n in range(0, value.shape[1], LANES)]


def spread(packed, f):
    parts = tiles(packed)
    cells = parts[3 * f : 3 * f + 3] + [pltpu.roll(parts[-1], LANES - REST * f, 1) if f else parts[-1]]
    lane = lane_ids(OWN)
    rows = []
    for row in range(ROWS):
        at, off = divmod(row * COLS, LANES)
        piece = cells[at]
        if off:
            piece = jnp.where(
                lane < LANES - off,
                pltpu.roll(piece, LANES - off, 1),
                pltpu.roll(cells[at + 1], LANES - off, 1),
            )
        rows.append(jnp.where(lane < COLS, piece, 0.0))
    return rows


def pack(frame, place):
    rows = tiles(frame)
    lane = lane_ids(frame.shape[0])
    pieces = []
    for at in range(MAIN // LANES):
        row, off = divmod(at * LANES, COLS)
        piece = pltpu.roll(rows[row], LANES - off, 1) if off else rows[row]
        pieces.append(jnp.where(lane < COLS - off, piece, pltpu.roll(rows[row + 1], COLS - off, 1)))
    row, off = divmod(MAIN, COLS)
    return jnp.concatenate(pieces, axis=1), pltpu.roll(rows[row], (LANES - off + REST * place) % LANES, 1)


def join(packs):
    lane = lane_ids(packs[0][0].shape[0])
    rest = jnp.zeros(packs[0][1].shape, F32)
    for place in range(len(packs) - 1, -1, -1):
        rest = jnp.where(lane < REST * (place + 1), packs[place][1], rest)
    return jnp.concatenate([main for main, _ in packs] + [rest], axis=1)


def pack_latent(lat):
    packs = []
    for f in range(FRAMES):
        frame = lat[f].astype(F32)
        rest = jnp.concatenate([frame[:, MAIN:], jnp.zeros((OWN, LANES - REST), F32)], axis=1)
        packs.append((frame[:, :MAIN], pltpu.roll(rest, REST * f, 1) if f else rest))
    return join(packs)


def kernel(
    sections,
    chans,
    lat_hbm,
    w1_hbm,
    w2_hbm,
    g1_hbm,
    b1_hbm,
    g2_hbm,
    b2_hbm,
    out_ref,
    lat,
    weights,
    vecs,
    flipped,
    values,
    squares,
    partial_all,
    turned,
    w_out,
    w_in,
    stacked,
    sums,
    own_sums,
    shares,
    shares_next,
    from_line,
    from_before,
    local_sem,
    all_send,
    all_recv,
    value_send,
    value_recv,
    w_send,
    w_recv,
    line_send,
    line_recv,
    next_send,
    next_recv,
    next_ready,
    ready,
):
    t = lax.axis_index("tm")
    chan = lax.axis_index("chan")
    x, y = lax.rem(chan, SIDE), lax.div(chan, SIDE)
    parity = lax.rem(t, 2)

    swap = [parity, 1 - parity]
    index_a = [x + s * (y - x) for s in swap]
    index_b = [y + s * (x - y) for s in swap]

    def chan_at(j, a, b):
        s = swap[j]
        return a * (1 + (SIDE - 1) * s) + b * (SIDE - (SIDE - 1) * s)

    def shifted(index, d):
        return lax.rem(index + d, SIDE)

    def a_peer(j, d):
        return (t, chan_at(j, shifted(index_a[j], d), index_b[j]))

    def b_peer(j, d, later=0):
        return (t + later, chan_at(j, index_a[j], shifted(index_b[j], d)))

    def remote(src, dst, send, recv, device):
        return pltpu.make_async_remote_copy(
            src_ref=src,
            dst_ref=dst,
            send_sem=send,
            recv_sem=recv,
            device_id=device,
            device_id_type=pl.DeviceIdType.MESH,
        )

    near, far, far_first = (1, 3), (2,), (2, 1, 3)

    loads = [
        pltpu.make_async_copy(lat_hbm, lat, local_sem.at[0]),
        pltpu.make_async_copy(w1_hbm, weights.at[0], local_sem.at[1]),
        pltpu.make_async_copy(w2_hbm, weights.at[1], local_sem.at[2]),
    ]
    for n, ref in enumerate((g1_hbm, b1_hbm, g2_hbm, b2_hbm)):
        loads.append(pltpu.make_async_copy(ref, vecs.at[n], local_sem.at[3 + n]))
    for load in loads:
        load.start()

    barrier = pltpu.get_barrier_semaphore()

    def tell(semaphore, device):
        pl.semaphore_signal(semaphore, inc=1, device_id=device, device_id_type=pl.DeviceIdType.MESH)

    def greet(device):
        tell(barrier, device)

    for d in (1, 2, 3):
        greet((t, SIDE * y + shifted(x, d)))
        greet((t, SIDE * shifted(y, d) + x))

    @pl.when(t < sections - 1)
    def _():
        greet((t + 1, chan))

    def own_squares(value):
        sums_of = jnp.sum(value * value, axis=0, keepdims=True)
        for n, part in enumerate(tiles(sums_of)):
            squares[n : n + 1, :] = part

    for n in range(4):
        loads[3 + n].wait()
    flipped[...] = jnp.zeros((LANES, LANES), F32)
    for n in range(4):
        flipped[n : n + 1, 0:OWN] = vecs[n]
    columns = jnp.transpose(flipped[...])[:OWN]

    def column(n):
        return jnp.broadcast_to(columns[:, n : n + 1], (OWN, LANES))

    bias = [column(1), column(3)]
    gain = [spread_lanes(column(0)), spread_lanes(column(2))]

    squares[...] = jnp.zeros((16, LANES), F32)
    loads[0].wait()
    value = pack_latent(lat)
    values[0, 0] = fold(value * gain[0])
    own_squares(value)
    partial_all[0, 0] = squares[...].astype(BF16)

    sends = []

    def start(copy):
        copy.start()
        sends.append(copy)

    def send_values(j, steps):
        for d in steps:
            start(
                remote(
                    values.at[j, 0],
                    values.at[j, SIDE - d],
                    value_send.at[j, d],
                    value_recv.at[j, SIDE - d],
                    a_peer(j, d),
                )
            )

    def wait_values(j, slot):
        remote(
            values.at[j, 0], values.at[j, slot], value_send.at[j, slot], value_recv.at[j, slot], a_peer(j, slot)
        ).wait_recv()

    def any_copy(j, di, dj):
        to = (SIDE - di) % SIDE * SIDE + (SIDE - dj) % SIDE
        return remote(
            partial_all.at[j, 0],
            partial_all.at[j, to],
            all_send.at[j, di * SIDE + dj],
            all_recv.at[j, to],
            (t, SIDE * shifted(y, dj) + shifted(x, di)),
        )

    others = sorted(
        [(di, dj) for di in range(SIDE) for dj in range(SIDE) if di or dj],
        key=lambda o: -min(o[0], SIDE - o[0]) - min(o[1], SIDE - o[1]),
    )

    def send_squares(j, diagonal):
        for di, dj in others:
            if bool(di and dj) == diagonal:
                start(any_copy(j, di, dj))

    def scales_all(j):
        total = partial_all[j, 0].astype(F32)
        for di, dj in others[::-1]:
            any_copy(j, SIDE - di if di else 0, SIDE - dj if dj else 0).wait_recv()
            total = total + partial_all[j, di * SIDE + dj].astype(F32)
        return lax.rsqrt(total / chans + 1e-06)

    def turn_weights(j):
        loads[1 + j].wait()
        for k in range(3):
            part = weights[j, 9 * k : 9 * k + 9].astype(F32).reshape(9 * OWN, chans)
            part = jnp.concatenate([part, jnp.zeros((DEPTH - 9 * OWN, chans), F32)], axis=0)
            flat = jnp.transpose(part)
            turned[...] = flat
            for d in range(SIDE):
                rows = []
                for e in range(SIDE):
                    block = chan_at(j, shifted(index_a[j], d), shifted(index_b[j], e))
                    rows.append(turned[pl.ds(pl.multiple_of(block * OWN, 8), OWN), :])
                rows = jnp.concatenate(rows, axis=0).astype(BF16)
                if d == 0:
                    w_in[j, 0, k] = rows
                else:
                    w_out[j, d - 1, k] = rows

    def send_weights(j, steps):
        for d in steps:
            start(
                remote(
                    w_out.at[j, d - 1],
                    w_in.at[j, SIDE - d],
                    w_send.at[j, d],
                    w_recv.at[j, SIDE - d],
                    a_peer(j, d),
                )
            )

    def stack_taps(slot, j, scale):
        normed = unfold(values[j, slot]) * jnp.concatenate([scale[n : n + 1] for n in range(PACKED // LANES)], axis=1)
        act = 0.5 * normed * (1.0 + jnp.tanh(0.5 * normed))
        act = act.astype(BF16).astype(F32)
        for f in range(FRAMES):
            rows = spread(act, f)
            shifts = [
                [pltpu.roll(r, 1, 1) for r in rows],
                rows,
                [pltpu.roll(r, LANES - 1, 1) for r in rows],
            ]
            none = jnp.zeros((OWN, LANES), F32)
            taps = []
            for dy in range(3):
                for dx in range(3):
                    moved = [none] + shifts[dx] + [none]
                    taps.append(jnp.concatenate(moved[dy : dy + ROWS], axis=1))
            taps.append(jnp.zeros((DEPTH - 9 * OWN, WIDE), F32))
            stacked[f, slot] = jnp.concatenate(taps, axis=0).astype(BF16)

    group = SIDE * OWN

    def emit_all(j, product):
        last = product(2)
        later = pack(last[:group], 1)
        sums[2, :group] = last[group : 2 * group]
        sums[2, group : 2 * group] = last[2 * group :]
        mid = product(1)
        later = join([pack(sums[2, :group] + mid[:group], 0), later])
        for e in range(SIDE):
            shares_next[j, e] = fold_next(later[e * OWN : (e + 1) * OWN])
        sums[2, group : 2 * group] += mid[group : 2 * group]
        sums[2, :group] = mid[2 * group :]

        @pl.when(t < sections - 1)
        def _():
            if j == 0:
                pl.semaphore_wait(next_ready, 1)
            for e in range(SIDE):
                next_copy(j, e).start()

        first = product(0)
        frames = [
            first[2 * group :],
            sums[2, :group] + first[group : 2 * group],
            sums[2, group : 2 * group] + first[:group],
        ]
        packed = join([pack(frame, f) for f, frame in enumerate(frames)])
        own_sums[...] = packed[:OWN]
        for e in range(1, SIDE):
            shares[j, e] = fold(packed[e * OWN : (e + 1) * OWN])
        for d in far_first:
            start(line_copy(j, d))

    def left_of(j, slot):
        return w_in[j, slot].reshape(3 * group, DEPTH)

    def wait_weights(j, slot):
        remote(
            w_out.at[j, 0], w_in.at[j, slot], w_send.at[j, slot], w_recv.at[j, slot], a_peer(j, slot)
        ).wait_recv()

    def convolve_as_weights_come(j):
        for slot in (0, 1, 3):
            if slot:
                wait_weights(j, slot)
            for f in range(3):
                part = jnp.dot(left_of(j, slot), stacked[f, slot], preferred_element_type=F32)
                if slot:
                    part = part + sums[f]
                sums[f] = part
        wait_weights(j, 2)
        emit_all(j, lambda f: sums[f] + jnp.dot(left_of(j, 2), stacked[f, 2], preferred_element_type=F32))

    def convolve(j):
        for slot in (1, 3, 2):
            wait_weights(j, slot)
        left = jnp.concatenate([left_of(j, s) for s in range(SIDE)], axis=1)
        emit_all(
            j, lambda f: jnp.dot(left, stacked[f].reshape(SIDE * DEPTH, WIDE), preferred_element_type=F32)
        )

    def next_copy(j, e):
        return remote(
            shares_next.at[j, e],
            from_before.at[j, e],
            next_send.at[j, e],
            next_recv.at[j, e],
            b_peer(j, e, 1),
        )

    def line_copy(j, d):
        return remote(
            shares.at[j, d],
            from_line.at[j, SIDE - d],
            line_send.at[j, d],
            line_recv.at[j, SIDE - d],
            b_peer(j, d),
        )

    def collect(j):
        @pl.when(t > 0)
        def _():
            for e in range(SIDE):
                remote(
                    from_before.at[j, e],
                    from_before.at[j, e],
                    next_send.at[j, e],
                    next_recv.at[j, e],
                    (t, chan_at(j, shifted(index_a[j], 1), index_b[j])),
                ).wait_recv()

        for d in (1, 3, 2):
            remote(
                from_line.at[j, d],
                from_line.at[j, d],
                line_send.at[j, d],
                line_recv.at[j, d],
                b_peer(j, d),
            ).wait_recv()
        total = own_sums[...] + spread_lanes(bias[j])
        for d in range(1, SIDE):
            total = total + unfold(from_line[j, d])
        before = unfold_next(from_before[j, 0])
        for e in range(1, SIDE):
            before = before + unfold_next(from_before[j, e])
        return jnp.concatenate(
            [
                total[:, : 2 * MAIN] + before[:, : 2 * MAIN],
                total[:, 2 * MAIN : 3 * MAIN],
                total[:, 3 * MAIN :] + before[:, 2 * MAIN :],
            ],
            axis=1,
        )

    @pl.when(t == 0)
    def _():
        from_before[...] = jnp.zeros(from_before.shape, BF16)

    turn_weights(0)
    pl.semaphore_wait(barrier, 6 + jnp.where(t > 0, 1, 0))
    for d in (1, 2, 3):
        tell(ready, (t, SIDE * y + shifted(x, d)))
    send_squares(0, False)
    send_values(0, far_first)
    send_weights(0, far)
    pl.semaphore_wait(ready, 3)
    send_squares(0, True)
    send_weights(0, near)

    @pl.when(t > 0)
    def _():
        tell(next_ready, (t - 1, chan))

    turn_weights(1)
    scale = scales_all(0)
    for slot in (0, 1, 3, 2):
        if slot:
            wait_values(0, slot)
        stack_taps(slot, 0, scale)
    convolve_as_weights_come(0)
    send_weights(1, far_first)

    middle = collect(0)
    rest = jnp.where(lane_ids(OWN) < FRAMES * REST, middle[:, FRAMES * MAIN :], 0.0)
    middle = jnp.concatenate([middle[:, : FRAMES * MAIN], rest], axis=1).astype(BF16).astype(F32)
    values[1, 0] = fold(middle * gain[1])
    own_squares(middle)
    partial_all[1, 0] = squares[...].astype(BF16)
    send_squares(1, True)
    send_squares(1, False)
    send_values(1, far_first)
    scale = scales_all(1)
    for slot in (0, 1, 3, 2):
        if slot:
            wait_values(1, slot)
        stack_taps(slot, 1, scale)
    convolve(1)
    result = pack_latent(lat) + collect(1)
    for f in range(FRAMES):
        rest = result[:, FRAMES * MAIN :]
        rest = pltpu.roll(rest, LANES - REST * f, 1) if f else rest
        frame = jnp.concatenate([result[:, f * MAIN : (f + 1) * MAIN], rest], axis=1)
        out_ref[f] = frame[:, : ROWS * COLS].astype(BF16)

    for copy in sends:
        copy.wait_send()

    @pl.when(t < sections - 1)
    def _():
        for j in range(2):
            for e in range(SIDE):
                next_copy(j, e).wait_send()


def block(sections, latent, gain_one, weight_one, bias_one, gain_two, weight_two, bias_two):
    frames = latent.shape[1]
    chans = weight_one.shape[3]
    dma = pltpu.SemaphoreType.DMA
    anywhere = pl.BlockSpec(memory_space=pltpu.HBM)
    result = pl.pallas_call(
        functools.partial(kernel, sections, chans),
        out_shape=jax.ShapeDtypeStruct((frames, OWN, ROWS * COLS), BF16),
        in_specs=[anywhere] * 7,
        out_specs=pl.BlockSpec(memory_space=pltpu.VMEM),
        scratch_shapes=[
            pltpu.VMEM((frames, OWN, ROWS * COLS), BF16),
            pltpu.VMEM((2, 27, OWN, chans), BF16),
            pltpu.VMEM((4, 1, OWN), F32),
            pltpu.VMEM((LANES, LANES), F32),
            pltpu.VMEM((2, SIDE, 2 * OWN, PACKED // 2), BF16),
            pltpu.VMEM((16, LANES), F32),
            pltpu.VMEM((2, SIDE * SIDE, 16, LANES), BF16),
            pltpu.VMEM((chans, DEPTH), F32),
            pltpu.VMEM((2, SIDE - 1, 3, SIDE * OWN, DEPTH), BF16),
            pltpu.VMEM((2, SIDE, 3, SIDE * OWN, DEPTH), BF16),
            pltpu.VMEM((frames, SIDE, DEPTH, WIDE), BF16),
            pltpu.VMEM((frames, 3 * SIDE * OWN, WIDE), F32),
            pltpu.VMEM((OWN, PACKED), F32),
            pltpu.VMEM((2, SIDE, 2 * OWN, PACKED // 2), BF16),
            pltpu.VMEM((2, SIDE, 16, NEXT_HALF), BF16),
            pltpu.VMEM((2, SIDE, 2 * OWN, PACKED // 2), BF16),
            pltpu.VMEM((2, SIDE, 16, NEXT_HALF), BF16),
            dma((7,)),
            dma((2, SIDE * SIDE)),
            dma((2, SIDE * SIDE)),
        ]
        + [dma((2, SIDE))] * 8
        + [pltpu.SemaphoreType.REGULAR] * 2,
        compiler_params=pltpu.CompilerParams(
            collective_id=0, has_side_effects=True, vmem_limit_bytes=40 * 1024 * 1024
        ),
    )(
        *[pltpu.with_memory_space_constraint(v, pltpu.HBM) for v in (
        jnp.transpose(latent, (1, 0, 2)),
        weight_one.reshape(27, OWN, chans),
        weight_two.reshape(27, OWN, chans),
        gain_one.reshape(1, OWN),
        bias_one.reshape(1, OWN),
        gain_two.reshape(1, OWN),
        bias_two.reshape(1, OWN),
    )]
    )
    return jnp.transpose(result, (1, 0, 2))


def solution(mesh):
    in_specs = (
        P("chan", "tm", None),
        P("chan"),
        P(None, None, "chan", None),
        P("chan"),
        P("chan"),
        P(None, None, "chan", None),
        P("chan"),
    )
    return jax.shard_map(
        functools.partial(block, mesh.shape["tm"]),
        mesh=mesh,
        in_specs=in_specs,
        out_specs=P("chan", "tm", None),
        check_vma=False,
    )
```

```python
import functools

import jax
import jax.numpy as jnp
from jax import lax
from jax.experimental import pallas as pl
from jax.experimental.pallas import tpu as pltpu
from jax.sharding import PartitionSpec as P

COLS = 104
ROWS = 4
LANES = 128
WIDE = ROWS * LANES
SIDE = 4
OWN = 24
FRAMES = 3
MAIN = 384
REST = ROWS * COLS - MAIN
PACKED = FRAMES * MAIN + LANES
DEPTH = 256
F32 = jnp.float32
BF16 = jnp.bfloat16


def unfold(value):
    value = value.astype(F32)
    return jnp.concatenate([value[:OWN], value[OWN:]], axis=1)


def fold(value):
    half = PACKED // 2
    return jnp.concatenate([value[:, :half], value[:, half:]], axis=0).astype(BF16)


def flat_half(width):
    return (OWN // 8 * width + LANES) // (2 * LANES) * LANES


def fold_next(value):
    width = value.shape[1]
    half = flat_half(width)
    parts = [value[8 * n : 8 * n + 8] for n in range(OWN // 8)]
    if 2 * half > OWN // 8 * width:
        parts.append(jnp.zeros((8, LANES), F32))
    flat = jnp.concatenate(parts, axis=1)
    return jnp.concatenate([flat[:, :half], flat[:, half:]], axis=0).astype(BF16)


def unfold_next(value, width):
    value = value.astype(F32)
    flat = jnp.concatenate([value[:8], value[8:]], axis=1)
    return jnp.concatenate([flat[:, width * n : width * (n + 1)] for n in range(OWN // 8)], axis=0)


def spread_lanes(value):
    return jnp.concatenate([value] * (PACKED // LANES), axis=1)


def lane_ids(rows):
    return lax.broadcasted_iota(jnp.int32, (rows, LANES), 1)


def tiles(value):
    return [value[:, n : n + LANES] for n in range(0, value.shape[1], LANES)]


def spread(packed, f):
    parts = tiles(packed)
    cells = parts[3 * f : 3 * f + 3] + [pltpu.roll(parts[-1], LANES - REST * f, 1) if f else parts[-1]]
    lane = lane_ids(OWN)
    rows = []
    for row in range(ROWS):
        at, off = divmod(row * COLS, LANES)
        piece = cells[at]
        if off:
            piece = jnp.where(
                lane < LANES - off,
                pltpu.roll(piece, LANES - off, 1),
                pltpu.roll(cells[at + 1], LANES - off, 1),
            )
        rows.append(jnp.where(lane < COLS, piece, 0.0))
    return rows


def pack(frame, place):
    rows = tiles(frame)
    lane = lane_ids(frame.shape[0])
    pieces = []
    for at in range(MAIN // LANES):
        row, off = divmod(at * LANES, COLS)
        piece = pltpu.roll(rows[row], LANES - off, 1) if off else rows[row]
        pieces.append(jnp.where(lane < COLS - off, piece, pltpu.roll(rows[row + 1], COLS - off, 1)))
    row, off = divmod(MAIN, COLS)
    return jnp.concatenate(pieces, axis=1), pltpu.roll(rows[row], (LANES - off + REST * place) % LANES, 1)


def join(packs):
    lane = lane_ids(packs[0][0].shape[0])
    rest = jnp.zeros(packs[0][1].shape, F32)
    for place in range(len(packs) - 1, -1, -1):
        rest = jnp.where(lane < REST * (place + 1), packs[place][1], rest)
    return jnp.concatenate([main for main, _ in packs] + [rest], axis=1)


def pack_latent(lat):
    packs = []
    for f in range(FRAMES):
        frame = lat[f].astype(F32)
        rest = jnp.concatenate([frame[:, MAIN:], jnp.zeros((OWN, LANES - REST), F32)], axis=1)
        packs.append((frame[:, :MAIN], pltpu.roll(rest, REST * f, 1) if f else rest))
    return join(packs)


def kernel(
    sections,
    chans,
    lat_hbm,
    w1_hbm,
    w2_hbm,
    g1_hbm,
    b1_hbm,
    g2_hbm,
    b2_hbm,
    out_ref,
    lat,
    weights,
    vecs,
    flipped,
    values,
    squares,
    partial_all,
    turned,
    w_out,
    w_in,
    stacked,
    sums,
    own_sums,
    shares,
    shares_far,
    shares_near,
    from_line,
    before_far,
    before_near,
    local_sem,
    all_send,
    all_recv,
    value_send,
    value_recv,
    w_send,
    w_recv,
    line_send,
    line_recv,
    next_send,
    next_recv,
    next_ready,
    ready,
):
    t = lax.axis_index("tm")
    chan = lax.axis_index("chan")
    x, y = lax.rem(chan, SIDE), lax.div(chan, SIDE)
    parity = lax.rem(t, 2)

    swap = [parity, 1 - parity]
    index_a = [x + s * (y - x) for s in swap]
    index_b = [y + s * (x - y) for s in swap]

    def chan_at(j, a, b):
        s = swap[j]
        return a * (1 + (SIDE - 1) * s) + b * (SIDE - (SIDE - 1) * s)

    def shifted(index, d):
        return lax.rem(index + d, SIDE)

    def a_peer(j, d):
        return (t, chan_at(j, shifted(index_a[j], d), index_b[j]))

    def b_peer(j, d, later=0):
        return (t + later, chan_at(j, index_a[j], shifted(index_b[j], d)))

    def remote(src, dst, send, recv, device):
        return pltpu.make_async_remote_copy(
            src_ref=src,
            dst_ref=dst,
            send_sem=send,
            recv_sem=recv,
            device_id=device,
            device_id_type=pl.DeviceIdType.MESH,
        )

    near, far, far_first, next_order = (1, 3), (2,), (2, 1, 3), (2, 1, 3, 0)

    loads = [
        pltpu.make_async_copy(lat_hbm, lat, local_sem.at[0]),
        pltpu.make_async_copy(w1_hbm, weights.at[0], local_sem.at[1]),
        pltpu.make_async_copy(w2_hbm, weights.at[1], local_sem.at[2]),
    ]
    for n, ref in enumerate((g1_hbm, b1_hbm, g2_hbm, b2_hbm)):
        loads.append(pltpu.make_async_copy(ref, vecs.at[n], local_sem.at[3 + n]))
    for load in loads:
        load.start()

    barrier = pltpu.get_barrier_semaphore()

    def tell(semaphore, device):
        pl.semaphore_signal(semaphore, inc=1, device_id=device, device_id_type=pl.DeviceIdType.MESH)

    def greet(device):
        tell(barrier, device)

    for d in (1, 2, 3):
        greet((t, SIDE * y + shifted(x, d)))
        greet((t, SIDE * shifted(y, d) + x))

    @pl.when(t < sections - 1)
    def _():
        greet((t + 1, chan))

    def own_squares(value):
        sums_of = jnp.sum(value * value, axis=0, keepdims=True)
        for n, part in enumerate(tiles(sums_of)):
            squares[n : n + 1, :] = part

    for n in range(4):
        loads[3 + n].wait()
    flipped[...] = jnp.zeros((LANES, LANES), F32)
    for n in range(4):
        flipped[n : n + 1, 0:OWN] = vecs[n]
    columns = jnp.transpose(flipped[...])[:OWN]

    def column(n):
        return jnp.broadcast_to(columns[:, n : n + 1], (OWN, LANES))

    bias = [column(1), column(3)]
    gain = [spread_lanes(column(0)), spread_lanes(column(2))]

    squares[...] = jnp.zeros((16, LANES), F32)
    loads[0].wait()
    value = pack_latent(lat)
    values[0, 0] = fold(value * gain[0])
    own_squares(value)
    partial_all[0, 0] = squares[...].astype(BF16)

    sends = []

    def start(copy):
        copy.start()
        sends.append(copy)

    def send_values(j, steps):
        for d in steps:
            start(
                remote(
                    values.at[j, 0],
                    values.at[j, SIDE - d],
                    value_send.at[j, d],
                    value_recv.at[j, SIDE - d],
                    a_peer(j, d),
                )
            )

    def wait_values(j, slot):
        remote(
            values.at[j, 0], values.at[j, slot], value_send.at[j, slot], value_recv.at[j, slot], a_peer(j, slot)
        ).wait_recv()

    def any_copy(j, di, dj):
        to = (SIDE - di) % SIDE * SIDE + (SIDE - dj) % SIDE
        return remote(
            partial_all.at[j, 0],
            partial_all.at[j, to],
            all_send.at[j, di * SIDE + dj],
            all_recv.at[j, to],
            (t, SIDE * shifted(y, dj) + shifted(x, di)),
        )

    others = sorted(
        [(di, dj) for di in range(SIDE) for dj in range(SIDE) if di or dj],
        key=lambda o: -min(o[0], SIDE - o[0]) - min(o[1], SIDE - o[1]),
    )

    def send_squares(j, diagonal):
        for di, dj in others:
            if bool(di and dj) == diagonal:
                start(any_copy(j, di, dj))

    def scales_all(j):
        total = partial_all[j, 0].astype(F32)
        for di, dj in others[::-1]:
            any_copy(j, SIDE - di if di else 0, SIDE - dj if dj else 0).wait_recv()
            total = total + partial_all[j, di * SIDE + dj].astype(F32)
        return lax.rsqrt(total / chans + 1e-06)

    def turn_weights(j):
        loads[1 + j].wait()
        for k in range(3):
            part = weights[j, 9 * k : 9 * k + 9].astype(F32).reshape(9 * OWN, chans)
            part = jnp.concatenate([part, jnp.zeros((DEPTH - 9 * OWN, chans), F32)], axis=0)
            flat = jnp.transpose(part)
            turned[...] = flat
            for d in range(SIDE):
                rows = []
                for e in range(SIDE):
                    block = chan_at(j, shifted(index_a[j], d), shifted(index_b[j], e))
                    rows.append(turned[pl.ds(pl.multiple_of(block * OWN, 8), OWN), :])
                rows = jnp.concatenate(rows, axis=0).astype(BF16)
                if d == 0:
                    w_in[j, 0, k] = rows
                else:
                    w_out[j, d - 1, k] = rows

    def send_weights(j, steps):
        for d in steps:
            start(
                remote(
                    w_out.at[j, d - 1],
                    w_in.at[j, SIDE - d],
                    w_send.at[j, d],
                    w_recv.at[j, SIDE - d],
                    a_peer(j, d),
                )
            )

    def stack_taps(slot, j, scale):
        normed = unfold(values[j, slot]) * jnp.concatenate([scale[n : n + 1] for n in range(PACKED // LANES)], axis=1)
        act = 0.5 * normed * (1.0 + jnp.tanh(0.5 * normed))
        act = act.astype(BF16).astype(F32)
        for f in range(FRAMES):
            rows = spread(act, f)
            shifts = [
                [pltpu.roll(r, 1, 1) for r in rows],
                rows,
                [pltpu.roll(r, LANES - 1, 1) for r in rows],
            ]
            none = jnp.zeros((OWN, LANES), F32)
            taps = []
            for dy in range(3):
                for dx in range(3):
                    moved = [none] + shifts[dx] + [none]
                    taps.append(jnp.concatenate(moved[dy : dy + ROWS], axis=1))
            taps.append(jnp.zeros((DEPTH - 9 * OWN, WIDE), F32))
            stacked[f, slot] = jnp.concatenate(taps, axis=0).astype(BF16)

    group = SIDE * OWN

    def emit_all(j, product):
        last = product(2)
        main, rest = pack(last[:group], 1)
        for e in range(SIDE):
            shares_far[j, e] = fold_next(main[e * OWN : (e + 1) * OWN])

        @pl.when(t < sections - 1)
        def _():
            if j == 0:
                pl.semaphore_wait(next_ready, 1)
            for e in next_order:
                next_copy(j, e, 0).start()

        sums[2, :group] = last[group : 2 * group]
        sums[2, group : 2 * group] = last[2 * group :]
        mid = product(1)
        nearer, its_rest = pack(sums[2, :group] + mid[:group], 0)
        lane = lane_ids(group)
        rest = jnp.where(lane < REST, its_rest, jnp.where(lane < 2 * REST, rest, 0.0))
        nearer = jnp.concatenate([nearer, rest], axis=1)
        for e in range(SIDE):
            shares_near[j, e] = fold_next(nearer[e * OWN : (e + 1) * OWN])

        @pl.when(t < sections - 1)
        def _():
            for e in next_order:
                next_copy(j, e, 1).start()

        sums[2, group : 2 * group] += mid[group : 2 * group]
        sums[2, :group] = mid[2 * group :]
        first = product(0)
        frames = [
            first[2 * group :],
            sums[2, :group] + first[group : 2 * group],
            sums[2, group : 2 * group] + first[:group],
        ]
        packed = join([pack(frame, f) for f, frame in enumerate(frames)])
        own_sums[...] = packed[:OWN]
        for e in range(1, SIDE):
            shares[j, e] = fold(packed[e * OWN : (e + 1) * OWN])
        for d in far_first:
            start(line_copy(j, d))

    def left_of(j, slot):
        return w_in[j, slot].reshape(3 * group, DEPTH)

    def wait_weights(j, slot):
        remote(
            w_out.at[j, 0], w_in.at[j, slot], w_send.at[j, slot], w_recv.at[j, slot], a_peer(j, slot)
        ).wait_recv()

    def convolve_as_weights_come(j):
        for slot in (0, 1, 3):
            if slot:
                wait_weights(j, slot)
            for f in range(3):
                part = jnp.dot(left_of(j, slot), stacked[f, slot], preferred_element_type=F32)
                if slot:
                    part = part + sums[f]
                sums[f] = part
        wait_weights(j, 2)
        emit_all(j, lambda f: sums[f] + jnp.dot(left_of(j, 2), stacked[f, 2], preferred_element_type=F32))

    def convolve(j):
        for slot in (1, 3, 2):
            wait_weights(j, slot)
        left = jnp.concatenate([left_of(j, s) for s in range(SIDE)], axis=1)
        emit_all(
            j, lambda f: jnp.dot(left, stacked[f].reshape(SIDE * DEPTH, WIDE), preferred_element_type=F32)
        )

    def next_copy(j, e, part):
        return remote(
            (shares_far, shares_near)[part].at[j, e],
            (before_far, before_near)[part].at[j, e],
            next_send.at[j, part, e],
            next_recv.at[j, part, e],
            b_peer(j, e, 1),
        )

    def line_copy(j, d):
        return remote(
            shares.at[j, d],
            from_line.at[j, SIDE - d],
            line_send.at[j, d],
            line_recv.at[j, SIDE - d],
            b_peer(j, d),
        )

    def collect(j):
        @pl.when(t > 0)
        def _():
            for part, landed in enumerate((before_far, before_near)):
                for e in range(SIDE):
                    remote(
                        landed.at[j, e],
                        landed.at[j, e],
                        next_send.at[j, part, e],
                        next_recv.at[j, part, e],
                        (t, chan_at(j, shifted(index_a[j], 1), index_b[j])),
                    ).wait_recv()

        for d in (1, 3, 2):
            remote(
                from_line.at[j, d],
                from_line.at[j, d],
                line_send.at[j, d],
                line_recv.at[j, d],
                b_peer(j, d),
            ).wait_recv()
        total = own_sums[...] + spread_lanes(bias[j])
        for d in range(1, SIDE):
            total = total + unfold(from_line[j, d])
        second = unfold_next(before_far[j, 0], MAIN)
        first = unfold_next(before_near[j, 0], MAIN + LANES)
        for e in range(1, SIDE):
            second = second + unfold_next(before_far[j, e], MAIN)
            first = first + unfold_next(before_near[j, e], MAIN + LANES)
        return jnp.concatenate(
            [
                total[:, :MAIN] + first[:, :MAIN],
                total[:, MAIN : 2 * MAIN] + second,
                total[:, 2 * MAIN : 3 * MAIN],
                total[:, 3 * MAIN :] + first[:, MAIN:],
            ],
            axis=1,
        )

    @pl.when(t == 0)
    def _():
        before_far[...] = jnp.zeros(before_far.shape, BF16)
        before_near[...] = jnp.zeros(before_near.shape, BF16)

    turn_weights(0)
    pl.semaphore_wait(barrier, 6 + jnp.where(t > 0, 1, 0))
    for d in (1, 2, 3):
        tell(ready, (t, SIDE * y + shifted(x, d)))
    send_squares(0, False)
    send_values(0, far_first)
    send_weights(0, far)
    pl.semaphore_wait(ready, 3)
    send_squares(0, True)
    send_weights(0, near)

    @pl.when(t > 0)
    def _():
        tell(next_ready, (t - 1, chan))

    turn_weights(1)
    scale = scales_all(0)
    for slot in (0, 1, 3, 2):
        if slot:
            wait_values(0, slot)
        stack_taps(slot, 0, scale)
    convolve_as_weights_come(0)
    send_weights(1, far_first)

    middle = collect(0)
    rest = jnp.where(lane_ids(OWN) < FRAMES * REST, middle[:, FRAMES * MAIN :], 0.0)
    middle = jnp.concatenate([middle[:, : FRAMES * MAIN], rest], axis=1).astype(BF16).astype(F32)
    values[1, 0] = fold(middle * gain[1])
    own_squares(middle)
    partial_all[1, 0] = squares[...].astype(BF16)
    send_squares(1, True)
    send_squares(1, False)
    send_values(1, far_first)
    scale = scales_all(1)
    for slot in (0, 1, 3, 2):
        if slot:
            wait_values(1, slot)
        stack_taps(slot, 1, scale)
    convolve(1)
    result = pack_latent(lat) + collect(1)
    for f in range(FRAMES):
        rest = result[:, FRAMES * MAIN :]
        rest = pltpu.roll(rest, LANES - REST * f, 1) if f else rest
        frame = jnp.concatenate([result[:, f * MAIN : (f + 1) * MAIN], rest], axis=1)
        out_ref[f] = frame[:, : ROWS * COLS].astype(BF16)

    for copy in sends:
        copy.wait_send()

    @pl.when(t < sections - 1)
    def _():
        for j in range(2):
            for e in range(SIDE):
                for part in range(2):
                    next_copy(j, e, part).wait_send()


def block(sections, latent, gain_one, weight_one, bias_one, gain_two, weight_two, bias_two):
    frames = latent.shape[1]
    chans = weight_one.shape[3]
    dma = pltpu.SemaphoreType.DMA
    anywhere = pl.BlockSpec(memory_space=pltpu.HBM)
    result = pl.pallas_call(
        functools.partial(kernel, sections, chans),
        out_shape=jax.ShapeDtypeStruct((frames, OWN, ROWS * COLS), BF16),
        in_specs=[anywhere] * 7,
        out_specs=pl.BlockSpec(memory_space=pltpu.VMEM),
        scratch_shapes=[
            pltpu.VMEM((frames, OWN, ROWS * COLS), BF16),
            pltpu.VMEM((2, 27, OWN, chans), BF16),
            pltpu.VMEM((4, 1, OWN), F32),
            pltpu.VMEM((LANES, LANES), F32),
            pltpu.VMEM((2, SIDE, 2 * OWN, PACKED // 2), BF16),
            pltpu.VMEM((16, LANES), F32),
            pltpu.VMEM((2, SIDE * SIDE, 16, LANES), BF16),
            pltpu.VMEM((chans, DEPTH), F32),
            pltpu.VMEM((2, SIDE - 1, 3, SIDE * OWN, DEPTH), BF16),
            pltpu.VMEM((2, SIDE, 3, SIDE * OWN, DEPTH), BF16),
            pltpu.VMEM((frames, SIDE, DEPTH, WIDE), BF16),
            pltpu.VMEM((frames, 3 * SIDE * OWN, WIDE), F32),
            pltpu.VMEM((OWN, PACKED), F32),
            pltpu.VMEM((2, SIDE, 2 * OWN, PACKED // 2), BF16),
            pltpu.VMEM((2, SIDE, 16, flat_half(MAIN)), BF16),
            pltpu.VMEM((2, SIDE, 16, flat_half(MAIN + LANES)), BF16),
            pltpu.VMEM((2, SIDE, 2 * OWN, PACKED // 2), BF16),
            pltpu.VMEM((2, SIDE, 16, flat_half(MAIN)), BF16),
            pltpu.VMEM((2, SIDE, 16, flat_half(MAIN + LANES)), BF16),
            dma((7,)),
            dma((2, SIDE * SIDE)),
            dma((2, SIDE * SIDE)),
        ]
        + [dma((2, SIDE))] * 6
        + [dma((2, 2, SIDE))] * 2
        + [pltpu.SemaphoreType.REGULAR] * 2,
        compiler_params=pltpu.CompilerParams(
            collective_id=0, has_side_effects=True, vmem_limit_bytes=40 * 1024 * 1024
        ),
    )(
        *[pltpu.with_memory_space_constraint(v, pltpu.HBM) for v in (
        jnp.transpose(latent, (1, 0, 2)),
        weight_one.reshape(27, OWN, chans),
        weight_two.reshape(27, OWN, chans),
        gain_one.reshape(1, OWN),
        bias_one.reshape(1, OWN),
        gain_two.reshape(1, OWN),
        bias_two.reshape(1, OWN),
    )]
    )
    return jnp.transpose(result, (1, 0, 2))


def solution(mesh):
    in_specs = (
        P("chan", "tm", None),
        P("chan"),
        P(None, None, "chan", None),
        P("chan"),
        P("chan"),
        P(None, None, "chan", None),
        P("chan"),
    )
    return jax.shard_map(
        functools.partial(block, mesh.shape["tm"]),
        mesh=mesh,
        in_specs=in_specs,
        out_specs=P("chan", "tm", None),
        check_vma=False,
    )
```

```python
import functools

import jax
import jax.numpy as jnp
from jax import lax
from jax.experimental import pallas as pl
from jax.experimental.pallas import tpu as pltpu
from jax.sharding import PartitionSpec as P

COLS = 104
ROWS = 4
LANES = 128
WIDE = ROWS * LANES
SIDE = 4
OWN = 24
FRAMES = 3
MAIN = 384
REST = ROWS * COLS - MAIN
PACKED = FRAMES * MAIN + LANES
DEPTH = 256
F32 = jnp.float32
BF16 = jnp.bfloat16


def unfold(value):
    value = value.astype(F32)
    return jnp.concatenate([value[:OWN], value[OWN:]], axis=1)


def fold(value):
    half = PACKED // 2
    return jnp.concatenate([value[:, :half], value[:, half:]], axis=0).astype(BF16)


def flat_half(width):
    return (OWN // 8 * width + LANES) // (2 * LANES) * LANES


def fold_next(value):
    width = value.shape[1]
    half = flat_half(width)
    parts = [value[8 * n : 8 * n + 8] for n in range(OWN // 8)]
    if 2 * half > OWN // 8 * width:
        parts.append(jnp.zeros((8, LANES), F32))
    flat = jnp.concatenate(parts, axis=1)
    return jnp.concatenate([flat[:, :half], flat[:, half:]], axis=0).astype(BF16)


def unfold_next(value, width):
    value = value.astype(F32)
    flat = jnp.concatenate([value[:8], value[8:]], axis=1)
    return jnp.concatenate([flat[:, width * n : width * (n + 1)] for n in range(OWN // 8)], axis=0)


def spread_lanes(value):
    return jnp.concatenate([value] * (PACKED // LANES), axis=1)


def lane_ids(rows):
    return lax.broadcasted_iota(jnp.int32, (rows, LANES), 1)


def tiles(value):
    return [value[:, n : n + LANES] for n in range(0, value.shape[1], LANES)]


def spread(packed, f):
    parts = tiles(packed)
    cells = parts[3 * f : 3 * f + 3] + [pltpu.roll(parts[-1], LANES - REST * f, 1) if f else parts[-1]]
    lane = lane_ids(OWN)
    rows = []
    for row in range(ROWS):
        at, off = divmod(row * COLS, LANES)
        piece = cells[at]
        if off:
            piece = jnp.where(
                lane < LANES - off,
                pltpu.roll(piece, LANES - off, 1),
                pltpu.roll(cells[at + 1], LANES - off, 1),
            )
        rows.append(jnp.where(lane < COLS, piece, 0.0))
    return rows


def pack(frame, place):
    rows = tiles(frame)
    lane = lane_ids(frame.shape[0])
    pieces = []
    for at in range(MAIN // LANES):
        row, off = divmod(at * LANES, COLS)
        piece = pltpu.roll(rows[row], LANES - off, 1) if off else rows[row]
        pieces.append(jnp.where(lane < COLS - off, piece, pltpu.roll(rows[row + 1], COLS - off, 1)))
    row, off = divmod(MAIN, COLS)
    return jnp.concatenate(pieces, axis=1), pltpu.roll(rows[row], (LANES - off + REST * place) % LANES, 1)


def join(packs):
    lane = lane_ids(packs[0][0].shape[0])
    rest = jnp.zeros(packs[0][1].shape, F32)
    for place in range(len(packs) - 1, -1, -1):
        rest = jnp.where(lane < REST * (place + 1), packs[place][1], rest)
    return jnp.concatenate([main for main, _ in packs] + [rest], axis=1)


def pack_latent(lat):
    packs = []
    for f in range(FRAMES):
        frame = lat[f].astype(F32)
        rest = jnp.concatenate([frame[:, MAIN:], jnp.zeros((OWN, LANES - REST), F32)], axis=1)
        packs.append((frame[:, :MAIN], pltpu.roll(rest, REST * f, 1) if f else rest))
    return join(packs)


def kernel(
    sections,
    chans,
    lat_hbm,
    w1_hbm,
    w2_hbm,
    g1_hbm,
    b1_hbm,
    g2_hbm,
    b2_hbm,
    out_ref,
    lat,
    weights,
    vecs,
    flipped,
    values,
    squares,
    partial_all,
    turned,
    w_out,
    w_in,
    stacked,
    sums,
    own_sums,
    shares,
    shares_far,
    shares_near,
    from_line,
    before_far,
    before_near,
    local_sem,
    all_send,
    all_recv,
    value_send,
    value_recv,
    w_send,
    w_recv,
    line_send,
    line_recv,
    next_send,
    next_recv,
    next_ready,
    ready,
):
    t = lax.axis_index("tm")
    chan = lax.axis_index("chan")
    x, y = lax.rem(chan, SIDE), lax.div(chan, SIDE)
    parity = lax.rem(t, 2)

    swap = [parity, 1 - parity]
    index_a = [x + s * (y - x) for s in swap]
    index_b = [y + s * (x - y) for s in swap]

    def chan_at(j, a, b):
        s = swap[j]
        return a * (1 + (SIDE - 1) * s) + b * (SIDE - (SIDE - 1) * s)

    def shifted(index, d):
        return lax.rem(index + d, SIDE)

    def a_peer(j, d):
        return (t, chan_at(j, shifted(index_a[j], d), index_b[j]))

    def b_peer(j, d, later=0):
        return (t + later, chan_at(j, index_a[j], shifted(index_b[j], d)))

    def remote(src, dst, send, recv, device):
        return pltpu.make_async_remote_copy(
            src_ref=src,
            dst_ref=dst,
            send_sem=send,
            recv_sem=recv,
            device_id=device,
            device_id_type=pl.DeviceIdType.MESH,
        )

    near, far, far_first, next_order = (1, 3), (2,), (2, 1, 3), (2, 1, 3, 0)

    loads = [
        pltpu.make_async_copy(lat_hbm, lat, local_sem.at[0]),
        pltpu.make_async_copy(w1_hbm, weights.at[0], local_sem.at[1]),
        pltpu.make_async_copy(w2_hbm, weights.at[1], local_sem.at[2]),
    ]
    for n, ref in enumerate((g1_hbm, b1_hbm, g2_hbm, b2_hbm)):
        loads.append(pltpu.make_async_copy(ref, vecs.at[n], local_sem.at[3 + n]))

    barrier = pltpu.get_barrier_semaphore()

    def tell(semaphore, device):
        pl.semaphore_signal(semaphore, inc=1, device_id=device, device_id_type=pl.DeviceIdType.MESH)

    def greet(device):
        tell(barrier, device)

    for d in far_first:
        greet((t, SIDE * y + shifted(x, d)))
        greet((t, SIDE * shifted(y, d) + x))

    @pl.when(t < sections - 1)
    def _():
        greet((t + 1, chan))

    for load in loads:
        load.start()

    def own_squares(value):
        sums_of = jnp.sum(value * value, axis=0, keepdims=True)
        for n, part in enumerate(tiles(sums_of)):
            squares[n : n + 1, :] = part

    for n in range(4):
        loads[3 + n].wait()
    flipped[...] = jnp.zeros((LANES, LANES), F32)
    for n in range(4):
        flipped[n : n + 1, 0:OWN] = vecs[n]
    columns = jnp.transpose(flipped[...])[:OWN]

    def column(n):
        return jnp.broadcast_to(columns[:, n : n + 1], (OWN, LANES))

    bias = [column(1), column(3)]
    gain = [spread_lanes(column(0)), spread_lanes(column(2))]

    squares[...] = jnp.zeros((16, LANES), F32)
    loads[0].wait()
    value = pack_latent(lat)
    values[0, 0] = fold(value * gain[0])
    own_squares(value)
    partial_all[0, 0] = squares[...].astype(BF16)

    sends = []

    def start(copy):
        copy.start()
        sends.append(copy)

    def drain():
        for copy in sends:
            copy.wait_send()
        sends.clear()

    def drain_next(j):
        @pl.when(t < sections - 1)
        def _():
            for e in range(SIDE):
                for part in range(2):
                    next_copy(j, e, part).wait_send()

    def send_values(j, steps):
        for d in steps:
            start(
                remote(
                    values.at[j, 0],
                    values.at[j, SIDE - d],
                    value_send.at[j, d],
                    value_recv.at[j, SIDE - d],
                    a_peer(j, d),
                )
            )

    def wait_values(j, slot):
        remote(
            values.at[j, 0], values.at[j, slot], value_send.at[j, slot], value_recv.at[j, slot], a_peer(j, slot)
        ).wait_recv()

    def any_copy(j, di, dj):
        to = (SIDE - di) % SIDE * SIDE + (SIDE - dj) % SIDE
        return remote(
            partial_all.at[j, 0],
            partial_all.at[j, to],
            all_send.at[j, di * SIDE + dj],
            all_recv.at[j, to],
            (t, SIDE * shifted(y, dj) + shifted(x, di)),
        )

    others = sorted(
        [(di, dj) for di in range(SIDE) for dj in range(SIDE) if di or dj],
        key=lambda o: -min(o[0], SIDE - o[0]) - min(o[1], SIDE - o[1]),
    )

    def send_squares(j, diagonal):
        for di, dj in others:
            if bool(di and dj) == diagonal:
                start(any_copy(j, di, dj))

    def scales_all(j):
        total = partial_all[j, 0].astype(F32)
        for di, dj in others[::-1]:
            any_copy(j, SIDE - di if di else 0, SIDE - dj if dj else 0).wait_recv()
            total = total + partial_all[j, di * SIDE + dj].astype(F32)
        return lax.rsqrt(total / chans + 1e-06)

    def turn_weights(j):
        loads[1 + j].wait()
        for k in range(3):
            part = weights[j, 9 * k : 9 * k + 9].astype(F32).reshape(9 * OWN, chans)
            part = jnp.concatenate([part, jnp.zeros((DEPTH - 9 * OWN, chans), F32)], axis=0)
            flat = jnp.transpose(part)
            turned[...] = flat
            for d in range(SIDE):
                rows = []
                for e in range(SIDE):
                    block = chan_at(j, shifted(index_a[j], d), shifted(index_b[j], e))
                    rows.append(turned[pl.ds(pl.multiple_of(block * OWN, 8), OWN), :])
                rows = jnp.concatenate(rows, axis=0).astype(BF16)
                if d == 0:
                    w_in[j, 0, k] = rows
                else:
                    w_out[j, d - 1, k] = rows

    def send_weights(j, steps):
        for d in steps:
            start(
                remote(
                    w_out.at[j, d - 1],
                    w_in.at[j, SIDE - d],
                    w_send.at[j, d],
                    w_recv.at[j, SIDE - d],
                    a_peer(j, d),
                )
            )

    def stack_taps(slot, j, scale):
        normed = unfold(values[j, slot]) * jnp.concatenate([scale[n : n + 1] for n in range(PACKED // LANES)], axis=1)
        act = 0.5 * normed * (1.0 + jnp.tanh(0.5 * normed))
        act = act.astype(BF16).astype(F32)
        for f in range(FRAMES):
            rows = spread(act, f)
            shifts = [
                [pltpu.roll(r, 1, 1) for r in rows],
                rows,
                [pltpu.roll(r, LANES - 1, 1) for r in rows],
            ]
            none = jnp.zeros((OWN, LANES), F32)
            taps = []
            for dy in range(3):
                for dx in range(3):
                    moved = [none] + shifts[dx] + [none]
                    taps.append(jnp.concatenate(moved[dy : dy + ROWS], axis=1))
            taps.append(jnp.zeros((DEPTH - 9 * OWN, WIDE), F32))
            stacked[f, slot] = jnp.concatenate(taps, axis=0).astype(BF16)

    group = SIDE * OWN

    def emit_all(j, product):
        last = product(2)
        main, rest = pack(last[:group], 1)
        for e in range(SIDE):
            shares_far[j, e] = fold_next(main[e * OWN : (e + 1) * OWN])

        @pl.when(t < sections - 1)
        def _():
            if j == 0:
                pl.semaphore_wait(next_ready, 1)
            for e in next_order:
                next_copy(j, e, 0).start()

        sums[2, :group] = last[group : 2 * group]
        sums[2, group : 2 * group] = last[2 * group :]
        mid = product(1)
        nearer, its_rest = pack(sums[2, :group] + mid[:group], 0)
        lane = lane_ids(group)
        rest = jnp.where(lane < REST, its_rest, jnp.where(lane < 2 * REST, rest, 0.0))
        nearer = jnp.concatenate([nearer, rest], axis=1)
        for e in range(SIDE):
            shares_near[j, e] = fold_next(nearer[e * OWN : (e + 1) * OWN])

        @pl.when(t < sections - 1)
        def _():
            for e in next_order:
                next_copy(j, e, 1).start()

        sums[2, group : 2 * group] += mid[group : 2 * group]
        sums[2, :group] = mid[2 * group :]
        first = product(0)
        frames = [
            first[2 * group :],
            sums[2, :group] + first[group : 2 * group],
            sums[2, group : 2 * group] + first[:group],
        ]
        packed = join([pack(frame, f) for f, frame in enumerate(frames)])
        own_sums[...] = packed[:OWN]
        for e in range(1, SIDE):
            shares[j, e] = fold(packed[e * OWN : (e + 1) * OWN])
        for d in far_first:
            start(line_copy(j, d))

    def left_of(j, slot):
        return w_in[j, slot].reshape(3 * group, DEPTH)

    def wait_weights(j, slot):
        remote(
            w_out.at[j, 0], w_in.at[j, slot], w_send.at[j, slot], w_recv.at[j, slot], a_peer(j, slot)
        ).wait_recv()

    def convolve_as_weights_come(j):
        for slot in (0, 2, 3):
            if slot:
                wait_weights(j, slot)
            for f in range(3):
                part = jnp.dot(left_of(j, slot), stacked[f, slot], preferred_element_type=F32)
                if slot:
                    part = part + sums[f]
                sums[f] = part
        wait_weights(j, 1)
        emit_all(j, lambda f: sums[f] + jnp.dot(left_of(j, 1), stacked[f, 1], preferred_element_type=F32))

    def convolve(j):
        for slot in (1, 3, 2):
            wait_weights(j, slot)
        left = jnp.concatenate([left_of(j, s) for s in range(SIDE)], axis=1)
        emit_all(
            j, lambda f: jnp.dot(left, stacked[f].reshape(SIDE * DEPTH, WIDE), preferred_element_type=F32)
        )

    def next_copy(j, e, part):
        return remote(
            (shares_far, shares_near)[part].at[j, e],
            (before_far, before_near)[part].at[j, e],
            next_send.at[j, part, e],
            next_recv.at[j, part, e],
            b_peer(j, e, 1),
        )

    def line_copy(j, d):
        return remote(
            shares.at[j, d],
            from_line.at[j, SIDE - d],
            line_send.at[j, d],
            line_recv.at[j, SIDE - d],
            b_peer(j, d),
        )

    def collect(j):
        @pl.when(t > 0)
        def _():
            for part, landed in enumerate((before_far, before_near)):
                for e in range(SIDE):
                    remote(
                        landed.at[j, e],
                        landed.at[j, e],
                        next_send.at[j, part, e],
                        next_recv.at[j, part, e],
                        (t, chan_at(j, shifted(index_a[j], 1), index_b[j])),
                    ).wait_recv()

        for d in (1, 3, 2):
            remote(
                from_line.at[j, d],
                from_line.at[j, d],
                line_send.at[j, d],
                line_recv.at[j, d],
                b_peer(j, d),
            ).wait_recv()
        total = own_sums[...] + spread_lanes(bias[j])
        for d in range(1, SIDE):
            total = total + unfold(from_line[j, d])
        second = unfold_next(before_far[j, 0], MAIN)
        first = unfold_next(before_near[j, 0], MAIN + LANES)
        for e in range(1, SIDE):
            second = second + unfold_next(before_far[j, e], MAIN)
            first = first + unfold_next(before_near[j, e], MAIN + LANES)
        return jnp.concatenate(
            [
                total[:, :MAIN] + first[:, :MAIN],
                total[:, MAIN : 2 * MAIN] + second,
                total[:, 2 * MAIN : 3 * MAIN],
                total[:, 3 * MAIN :] + first[:, MAIN:],
            ],
            axis=1,
        )

    @pl.when(t == 0)
    def _():
        before_far[...] = jnp.zeros(before_far.shape, BF16)
        before_near[...] = jnp.zeros(before_near.shape, BF16)

    turn_weights(0)
    pl.semaphore_wait(barrier, 6 + jnp.where(t > 0, 1, 0))
    for d in (1, 2, 3):
        tell(ready, (t, SIDE * y + shifted(x, d)))
    send_squares(0, False)
    send_values(0, far_first)
    send_weights(0, far)
    pl.semaphore_wait(ready, 3)
    send_squares(0, True)
    send_weights(0, near)

    @pl.when(t > 0)
    def _():
        tell(next_ready, (t - 1, chan))

    turn_weights(1)
    scale = scales_all(0)
    for slot in (0, 1, 3, 2):
        if slot:
            wait_values(0, slot)
        stack_taps(slot, 0, scale)
    early = list(sends)
    sends.clear()
    convolve_as_weights_come(0)
    send_weights(1, far_first)

    middle = collect(0)
    rest = jnp.where(lane_ids(OWN) < FRAMES * REST, middle[:, FRAMES * MAIN :], 0.0)
    middle = jnp.concatenate([middle[:, : FRAMES * MAIN], rest], axis=1).astype(BF16).astype(F32)
    values[1, 0] = fold(middle * gain[1])
    own_squares(middle)
    partial_all[1, 0] = squares[...].astype(BF16)
    send_squares(1, False)
    send_squares(1, True)
    send_values(1, far_first)
    for copy in early:
        copy.wait_send()
    scale = scales_all(1)
    for slot in (0, 1, 3, 2):
        if slot:
            wait_values(1, slot)
        stack_taps(slot, 1, scale)
    middle_sends = list(sends)
    sends.clear()
    convolve(1)
    for copy in middle_sends:
        copy.wait_send()
    drain_next(0)
    result = pack_latent(lat) + collect(1)
    for f in range(FRAMES):
        rest = result[:, FRAMES * MAIN :]
        rest = pltpu.roll(rest, LANES - REST * f, 1) if f else rest
        frame = jnp.concatenate([result[:, f * MAIN : (f + 1) * MAIN], rest], axis=1)
        out_ref[f] = frame[:, : ROWS * COLS].astype(BF16)

    drain()
    drain_next(1)


def block(sections, latent, gain_one, weight_one, bias_one, gain_two, weight_two, bias_two):
    frames = latent.shape[1]
    chans = weight_one.shape[3]
    dma = pltpu.SemaphoreType.DMA
    anywhere = pl.BlockSpec(memory_space=pltpu.HBM)
    result = pl.pallas_call(
        functools.partial(kernel, sections, chans),
        out_shape=jax.ShapeDtypeStruct((frames, OWN, ROWS * COLS), BF16),
        in_specs=[anywhere] * 7,
        out_specs=pl.BlockSpec(memory_space=pltpu.VMEM),
        scratch_shapes=[
            pltpu.VMEM((frames, OWN, ROWS * COLS), BF16),
            pltpu.VMEM((2, 27, OWN, chans), BF16),
            pltpu.VMEM((4, 1, OWN), F32),
            pltpu.VMEM((LANES, LANES), F32),
            pltpu.VMEM((2, SIDE, 2 * OWN, PACKED // 2), BF16),
            pltpu.VMEM((16, LANES), F32),
            pltpu.VMEM((2, SIDE * SIDE, 16, LANES), BF16),
            pltpu.VMEM((chans, DEPTH), F32),
            pltpu.VMEM((2, SIDE - 1, 3, SIDE * OWN, DEPTH), BF16),
            pltpu.VMEM((2, SIDE, 3, SIDE * OWN, DEPTH), BF16),
            pltpu.VMEM((frames, SIDE, DEPTH, WIDE), BF16),
            pltpu.VMEM((frames, 3 * SIDE * OWN, WIDE), F32),
            pltpu.VMEM((OWN, PACKED), F32),
            pltpu.VMEM((2, SIDE, 2 * OWN, PACKED // 2), BF16),
            pltpu.VMEM((2, SIDE, 16, flat_half(MAIN)), BF16),
            pltpu.VMEM((2, SIDE, 16, flat_half(MAIN + LANES)), BF16),
            pltpu.VMEM((2, SIDE, 2 * OWN, PACKED // 2), BF16),
            pltpu.VMEM((2, SIDE, 16, flat_half(MAIN)), BF16),
            pltpu.VMEM((2, SIDE, 16, flat_half(MAIN + LANES)), BF16),
            dma((7,)),
            dma((2, SIDE * SIDE)),
            dma((2, SIDE * SIDE)),
        ]
        + [dma((2, SIDE))] * 6
        + [dma((2, 2, SIDE))] * 2
        + [pltpu.SemaphoreType.REGULAR] * 2,
        compiler_params=pltpu.CompilerParams(
            collective_id=0, has_side_effects=True, vmem_limit_bytes=40 * 1024 * 1024
        ),
    )(
        *[pltpu.with_memory_space_constraint(v, pltpu.HBM) for v in (
        jnp.transpose(latent, (1, 0, 2)),
        weight_one.reshape(27, OWN, chans),
        weight_two.reshape(27, OWN, chans),
        gain_one.reshape(1, OWN),
        bias_one.reshape(1, OWN),
        gain_two.reshape(1, OWN),
        bias_two.reshape(1, OWN),
    )]
    )
    return jnp.transpose(result, (1, 0, 2))


def solution(mesh):
    in_specs = (
        P("chan", "tm", None),
        P("chan"),
        P(None, None, "chan", None),
        P("chan"),
        P("chan"),
        P(None, None, "chan", None),
        P("chan"),
    )
    return jax.shard_map(
        functools.partial(block, mesh.shape["tm"]),
        mesh=mesh,
        in_specs=in_specs,
        out_specs=P("chan", "tm", None),
        check_vma=False,
    )
```

```python
import functools

import jax
import jax.numpy as jnp
from jax import lax
from jax.experimental import pallas as pl
from jax.experimental.pallas import tpu as pltpu
from jax.sharding import PartitionSpec as P

COLS = 104
ROWS = 4
LANES = 128
WIDE = ROWS * LANES
SIDE = 4
OWN = 24
FRAMES = 3
MAIN = 384
REST = ROWS * COLS - MAIN
PACKED = FRAMES * MAIN + LANES
DEPTH = 256
F32 = jnp.float32
BF16 = jnp.bfloat16


def unfold(value):
    value = value.astype(F32)
    return jnp.concatenate([value[:OWN], value[OWN:]], axis=1)


def fold(value):
    half = PACKED // 2
    return jnp.concatenate([value[:, :half], value[:, half:]], axis=0).astype(BF16)


def flat_half(width):
    return (OWN // 8 * width + LANES) // (2 * LANES) * LANES


def fold_next(value):
    width = value.shape[1]
    half = flat_half(width)
    parts = [value[8 * n : 8 * n + 8] for n in range(OWN // 8)]
    if 2 * half > OWN // 8 * width:
        parts.append(jnp.zeros((8, LANES), F32))
    flat = jnp.concatenate(parts, axis=1)
    return jnp.concatenate([flat[:, :half], flat[:, half:]], axis=0).astype(BF16)


def unfold_next(value, width):
    value = value.astype(F32)
    flat = jnp.concatenate([value[:8], value[8:]], axis=1)
    return jnp.concatenate([flat[:, width * n : width * (n + 1)] for n in range(OWN // 8)], axis=0)


def spread_lanes(value):
    return jnp.concatenate([value] * (PACKED // LANES), axis=1)


def lane_ids(rows):
    return lax.broadcasted_iota(jnp.int32, (rows, LANES), 1)


def tiles(value):
    return [value[:, n : n + LANES] for n in range(0, value.shape[1], LANES)]


def spread(packed, f):
    parts = tiles(packed)
    cells = parts[3 * f : 3 * f + 3] + [pltpu.roll(parts[-1], LANES - REST * f, 1) if f else parts[-1]]
    lane = lane_ids(OWN)
    rows = []
    for row in range(ROWS):
        at, off = divmod(row * COLS, LANES)
        piece = cells[at]
        if off:
            piece = jnp.where(
                lane < LANES - off,
                pltpu.roll(piece, LANES - off, 1),
                pltpu.roll(cells[at + 1], LANES - off, 1),
            )
        rows.append(jnp.where(lane < COLS, piece, 0.0))
    return rows


def pack(frame, place):
    rows = tiles(frame)
    lane = lane_ids(frame.shape[0])
    pieces = []
    for at in range(MAIN // LANES):
        row, off = divmod(at * LANES, COLS)
        piece = pltpu.roll(rows[row], LANES - off, 1) if off else rows[row]
        pieces.append(jnp.where(lane < COLS - off, piece, pltpu.roll(rows[row + 1], COLS - off, 1)))
    row, off = divmod(MAIN, COLS)
    return jnp.concatenate(pieces, axis=1), pltpu.roll(rows[row], (LANES - off + REST * place) % LANES, 1)


def join(packs):
    lane = lane_ids(packs[0][0].shape[0])
    rest = jnp.zeros(packs[0][1].shape, F32)
    for place in range(len(packs) - 1, -1, -1):
        rest = jnp.where(lane < REST * (place + 1), packs[place][1], rest)
    return jnp.concatenate([main for main, _ in packs] + [rest], axis=1)


def pack_latent(lat):
    packs = []
    for f in range(FRAMES):
        frame = lat[f].astype(F32)
        rest = jnp.concatenate([frame[:, MAIN:], jnp.zeros((OWN, LANES - REST), F32)], axis=1)
        packs.append((frame[:, :MAIN], pltpu.roll(rest, REST * f, 1) if f else rest))
    return join(packs)


def kernel(
    sections,
    chans,
    lat_hbm,
    w1_hbm,
    w2_hbm,
    g1_hbm,
    b1_hbm,
    g2_hbm,
    b2_hbm,
    out_ref,
    lat,
    weights,
    vecs,
    flipped,
    values,
    squares,
    partial_all,
    turned,
    w_out,
    w_in,
    stacked,
    sums,
    own_sums,
    shares,
    shares_far,
    shares_near,
    from_line,
    before_far,
    before_near,
    local_sem,
    all_send,
    all_recv,
    value_send,
    value_recv,
    w_send,
    w_recv,
    line_send,
    line_recv,
    next_send,
    next_recv,
    next_ready,
    ready,
):
    t = lax.axis_index("tm")
    chan = lax.axis_index("chan")
    x, y = lax.rem(chan, SIDE), lax.div(chan, SIDE)
    parity = lax.rem(t, 2)

    swap = [parity, 1 - parity]
    index_a = [x + s * (y - x) for s in swap]
    index_b = [y + s * (x - y) for s in swap]

    def chan_at(j, a, b):
        s = swap[j]
        return a * (1 + (SIDE - 1) * s) + b * (SIDE - (SIDE - 1) * s)

    def shifted(index, d):
        return lax.rem(index + d, SIDE)

    def a_peer(j, d):
        return (t, chan_at(j, shifted(index_a[j], d), index_b[j]))

    def b_peer(j, d, later=0):
        return (t + later, chan_at(j, index_a[j], shifted(index_b[j], d)))

    def remote(src, dst, send, recv, device):
        return pltpu.make_async_remote_copy(
            src_ref=src,
            dst_ref=dst,
            send_sem=send,
            recv_sem=recv,
            device_id=device,
            device_id_type=pl.DeviceIdType.MESH,
        )

    near, far, far_first, next_order = (1, 3), (2,), (2, 1, 3), (2, 1, 3, 0)

    loads = [
        pltpu.make_async_copy(lat_hbm, lat, local_sem.at[0]),
        pltpu.make_async_copy(w1_hbm, weights.at[0], local_sem.at[1]),
        pltpu.make_async_copy(w2_hbm, weights.at[1], local_sem.at[2]),
    ]
    for n, ref in enumerate((g1_hbm, b1_hbm, g2_hbm, b2_hbm)):
        loads.append(pltpu.make_async_copy(ref, vecs.at[n], local_sem.at[3 + n]))

    barrier = pltpu.get_barrier_semaphore()

    def tell(semaphore, device):
        pl.semaphore_signal(semaphore, inc=1, device_id=device, device_id_type=pl.DeviceIdType.MESH)

    def greet(device):
        tell(barrier, device)

    for d in far_first:
        greet((t, SIDE * y + shifted(x, d)))
        greet((t, SIDE * shifted(y, d) + x))

    @pl.when(t < sections - 1)
    def _():
        greet((t + 1, chan))

    for load in loads:
        load.start()

    def own_squares(value):
        sums_of = jnp.sum(value * value, axis=0, keepdims=True)
        for n, part in enumerate(tiles(sums_of)):
            squares[n : n + 1, :] = part

    for n in range(4):
        loads[3 + n].wait()
    flipped[...] = jnp.zeros((LANES, LANES), F32)
    for n in range(4):
        flipped[n : n + 1, 0:OWN] = vecs[n]
    columns = jnp.transpose(flipped[...])[:OWN]

    def column(n):
        return jnp.broadcast_to(columns[:, n : n + 1], (OWN, LANES))

    bias = [column(1), column(3)]
    gain = [spread_lanes(column(0)), spread_lanes(column(2))]

    squares[...] = jnp.zeros((16, LANES), F32)
    loads[0].wait()
    value = pack_latent(lat)
    values[0, 0] = fold(value * gain[0])
    own_squares(value)
    partial_all[0, 0] = squares[...].astype(BF16)

    sends = []

    def start(copy):
        copy.start()
        sends.append(copy)

    def drain():
        for copy in sends:
            copy.wait_send()
        sends.clear()

    def drain_next(j):
        @pl.when(t < sections - 1)
        def _():
            for e in range(SIDE):
                for part in range(2):
                    next_copy(j, e, part).wait_send()

    def send_values(j, steps):
        for d in steps:
            start(
                remote(
                    values.at[j, 0],
                    values.at[j, SIDE - d],
                    value_send.at[j, d],
                    value_recv.at[j, SIDE - d],
                    a_peer(j, d),
                )
            )

    def wait_values(j, slot):
        remote(
            values.at[j, 0], values.at[j, slot], value_send.at[j, slot], value_recv.at[j, slot], a_peer(j, slot)
        ).wait_recv()

    def any_copy(j, di, dj):
        to = (SIDE - di) % SIDE * SIDE + (SIDE - dj) % SIDE
        return remote(
            partial_all.at[j, 0],
            partial_all.at[j, to],
            all_send.at[j, di * SIDE + dj],
            all_recv.at[j, to],
            (t, SIDE * shifted(y, dj) + shifted(x, di)),
        )

    others = sorted(
        [(di, dj) for di in range(SIDE) for dj in range(SIDE) if di or dj],
        key=lambda o: -min(o[0], SIDE - o[0]) - min(o[1], SIDE - o[1]),
    )

    def send_squares(j, diagonal):
        for di, dj in others:
            if bool(di and dj) == diagonal:
                start(any_copy(j, di, dj))

    def scales_all(j):
        total = partial_all[j, 0].astype(F32)
        for di, dj in others[::-1]:
            any_copy(j, SIDE - di if di else 0, SIDE - dj if dj else 0).wait_recv()
            total = total + partial_all[j, di * SIDE + dj].astype(F32)
        return lax.rsqrt(total / chans + 1e-06)

    def turn_weights(j):
        loads[1 + j].wait()
        for k in range(3):
            part = weights[j, 9 * k : 9 * k + 9].astype(F32).reshape(9 * OWN, chans)
            part = jnp.concatenate([part, jnp.zeros((DEPTH - 9 * OWN, chans), F32)], axis=0)
            flat = jnp.transpose(part)
            turned[...] = flat
            for d in range(SIDE):
                rows = []
                for e in range(SIDE):
                    block = chan_at(j, shifted(index_a[j], d), shifted(index_b[j], e))
                    rows.append(turned[pl.ds(pl.multiple_of(block * OWN, 8), OWN), :])
                rows = jnp.concatenate(rows, axis=0).astype(BF16)
                if d == 0:
                    w_in[j, 0, k] = rows
                else:
                    w_out[j, d - 1, k] = rows

    def send_weights(j, steps):
        for d in steps:
            start(
                remote(
                    w_out.at[j, d - 1],
                    w_in.at[j, SIDE - d],
                    w_send.at[j, d],
                    w_recv.at[j, SIDE - d],
                    a_peer(j, d),
                )
            )

    def stack_taps(slot, j, scale):
        normed = unfold(values[j, slot]) * jnp.concatenate([scale[n : n + 1] for n in range(PACKED // LANES)], axis=1)
        act = 0.5 * normed * (1.0 + jnp.tanh(0.5 * normed))
        act = act.astype(BF16).astype(F32)
        for f in range(FRAMES):
            rows = spread(act, f)
            shifts = [
                [pltpu.roll(r, 1, 1) for r in rows],
                rows,
                [pltpu.roll(r, LANES - 1, 1) for r in rows],
            ]
            none = jnp.zeros((OWN, LANES), F32)
            taps = []
            for dy in range(3):
                for dx in range(3):
                    moved = [none] + shifts[dx] + [none]
                    taps.append(jnp.concatenate(moved[dy : dy + ROWS], axis=1))
            taps.append(jnp.zeros((DEPTH - 9 * OWN, WIDE), F32))
            stacked[f, slot] = jnp.concatenate(taps, axis=0).astype(BF16)

    group = SIDE * OWN

    def emit_all(j, product):
        last = product(2)
        main, rest = pack(last[:group], 1)
        for e in range(SIDE):
            shares_far[j, e] = fold_next(main[e * OWN : (e + 1) * OWN])

        @pl.when(t < sections - 1)
        def _():
            if j == 0:
                pl.semaphore_wait(next_ready, 1)
            for e in next_order:
                next_copy(j, e, 0).start()

        sums[2, :group] = last[group : 2 * group]
        sums[2, group : 2 * group] = last[2 * group :]
        mid = product(1)
        nearer, its_rest = pack(sums[2, :group] + mid[:group], 0)
        lane = lane_ids(group)
        rest = jnp.where(lane < REST, its_rest, jnp.where(lane < 2 * REST, rest, 0.0))
        nearer = jnp.concatenate([nearer, rest], axis=1)
        for e in range(SIDE):
            shares_near[j, e] = fold_next(nearer[e * OWN : (e + 1) * OWN])

        @pl.when(t < sections - 1)
        def _():
            for e in next_order:
                next_copy(j, e, 1).start()

        sums[2, group : 2 * group] += mid[group : 2 * group]
        sums[2, :group] = mid[2 * group :]
        first = product(0)
        frames = [
            first[2 * group :],
            sums[2, :group] + first[group : 2 * group],
            sums[2, group : 2 * group] + first[:group],
        ]
        packed = join([pack(frame, f) for f, frame in enumerate(frames)])
        own_sums[...] = packed[:OWN]
        for e in range(1, SIDE):
            shares[j, e] = fold(packed[e * OWN : (e + 1) * OWN])
        for d in far_first:
            start(line_copy(j, d))

    def left_of(j, slot):
        return w_in[j, slot].reshape(3 * group, DEPTH)

    def wait_weights(j, slot):
        remote(
            w_out.at[j, 0], w_in.at[j, slot], w_send.at[j, slot], w_recv.at[j, slot], a_peer(j, slot)
        ).wait_recv()

    def convolve_as_weights_come(j):
        for slot in (0, 2, 3):
            if slot:
                wait_weights(j, slot)
            for f in range(3):
                part = jnp.dot(left_of(j, slot), stacked[f, slot], preferred_element_type=F32)
                if slot:
                    part = part + sums[f]
                sums[f] = part
        wait_weights(j, 1)
        emit_all(j, lambda f: sums[f] + jnp.dot(left_of(j, 1), stacked[f, 1], preferred_element_type=F32))

    def convolve(j):
        for slot in (1, 3, 2):
            wait_weights(j, slot)
        left = jnp.concatenate([left_of(j, s) for s in range(SIDE)], axis=1)
        emit_all(
            j, lambda f: jnp.dot(left, stacked[f].reshape(SIDE * DEPTH, WIDE), preferred_element_type=F32)
        )

    def next_copy(j, e, part):
        return remote(
            (shares_far, shares_near)[part].at[j, e],
            (before_far, before_near)[part].at[j, e],
            next_send.at[j, part, e],
            next_recv.at[j, part, e],
            b_peer(j, e, 1),
        )

    def line_copy(j, d):
        return remote(
            shares.at[j, d],
            from_line.at[j, SIDE - d],
            line_send.at[j, d],
            line_recv.at[j, SIDE - d],
            b_peer(j, d),
        )

    def collect(j):
        @pl.when(t > 0)
        def _():
            for part, landed in enumerate((before_far, before_near)):
                for e in range(SIDE):
                    remote(
                        landed.at[j, e],
                        landed.at[j, e],
                        next_send.at[j, part, e],
                        next_recv.at[j, part, e],
                        (t, chan_at(j, shifted(index_a[j], 1), index_b[j])),
                    ).wait_recv()

        for d in (1, 3, 2):
            remote(
                from_line.at[j, d],
                from_line.at[j, d],
                line_send.at[j, d],
                line_recv.at[j, d],
                b_peer(j, d),
            ).wait_recv()
        total = own_sums[...] + spread_lanes(bias[j])
        for d in range(1, SIDE):
            total = total + unfold(from_line[j, d])
        second = unfold_next(before_far[j, 0], MAIN)
        first = unfold_next(before_near[j, 0], MAIN + LANES)
        for e in range(1, SIDE):
            second = second + unfold_next(before_far[j, e], MAIN)
            first = first + unfold_next(before_near[j, e], MAIN + LANES)
        return jnp.concatenate(
            [
                total[:, :MAIN] + first[:, :MAIN],
                total[:, MAIN : 2 * MAIN] + second,
                total[:, 2 * MAIN : 3 * MAIN],
                total[:, 3 * MAIN :] + first[:, MAIN:],
            ],
            axis=1,
        )

    @pl.when(t == 0)
    def _():
        before_far[...] = jnp.zeros(before_far.shape, BF16)
        before_near[...] = jnp.zeros(before_near.shape, BF16)

    pl.semaphore_wait(barrier, 6 + jnp.where(t > 0, 1, 0))
    for d in (1, 2, 3):
        tell(ready, (t, SIDE * y + shifted(x, d)))
    send_squares(0, False)
    send_values(0, far_first)
    turn_weights(0)
    send_weights(0, far)
    pl.semaphore_wait(ready, 3)
    send_squares(0, True)
    send_weights(0, near)

    @pl.when(t > 0)
    def _():
        tell(next_ready, (t - 1, chan))

    turn_weights(1)
    scale = scales_all(0)
    for slot in (0, 1, 3, 2):
        if slot:
            wait_values(0, slot)
        stack_taps(slot, 0, scale)
    early = list(sends)
    sends.clear()
    convolve_as_weights_come(0)
    send_weights(1, far_first)

    middle = collect(0)
    rest = jnp.where(lane_ids(OWN) < FRAMES * REST, middle[:, FRAMES * MAIN :], 0.0)
    middle = jnp.concatenate([middle[:, : FRAMES * MAIN], rest], axis=1).astype(BF16).astype(F32)
    values[1, 0] = fold(middle * gain[1])
    own_squares(middle)
    partial_all[1, 0] = squares[...].astype(BF16)
    send_squares(1, False)
    send_squares(1, True)
    send_values(1, far_first)
    for copy in early:
        copy.wait_send()
    scale = scales_all(1)
    for slot in (0, 1, 3, 2):
        if slot:
            wait_values(1, slot)
        stack_taps(slot, 1, scale)
    middle_sends = list(sends)
    sends.clear()
    convolve(1)
    for copy in middle_sends:
        copy.wait_send()
    drain_next(0)
    result = pack_latent(lat) + collect(1)
    for f in range(FRAMES):
        rest = result[:, FRAMES * MAIN :]
        rest = pltpu.roll(rest, LANES - REST * f, 1) if f else rest
        frame = jnp.concatenate([result[:, f * MAIN : (f + 1) * MAIN], rest], axis=1)
        out_ref[f] = frame[:, : ROWS * COLS].astype(BF16)

    drain()
    drain_next(1)


def block(sections, latent, gain_one, weight_one, bias_one, gain_two, weight_two, bias_two):
    frames = latent.shape[1]
    chans = weight_one.shape[3]
    dma = pltpu.SemaphoreType.DMA
    anywhere = pl.BlockSpec(memory_space=pltpu.HBM)
    result = pl.pallas_call(
        functools.partial(kernel, sections, chans),
        out_shape=jax.ShapeDtypeStruct((frames, OWN, ROWS * COLS), BF16),
        in_specs=[anywhere] * 7,
        out_specs=pl.BlockSpec(memory_space=pltpu.VMEM),
        scratch_shapes=[
            pltpu.VMEM((frames, OWN, ROWS * COLS), BF16),
            pltpu.VMEM((2, 27, OWN, chans), BF16),
            pltpu.VMEM((4, 1, OWN), F32),
            pltpu.VMEM((LANES, LANES), F32),
            pltpu.VMEM((2, SIDE, 2 * OWN, PACKED // 2), BF16),
            pltpu.VMEM((16, LANES), F32),
            pltpu.VMEM((2, SIDE * SIDE, 16, LANES), BF16),
            pltpu.VMEM((chans, DEPTH), F32),
            pltpu.VMEM((2, SIDE - 1, 3, SIDE * OWN, DEPTH), BF16),
            pltpu.VMEM((2, SIDE, 3, SIDE * OWN, DEPTH), BF16),
            pltpu.VMEM((frames, SIDE, DEPTH, WIDE), BF16),
            pltpu.VMEM((frames, 3 * SIDE * OWN, WIDE), F32),
            pltpu.VMEM((OWN, PACKED), F32),
            pltpu.VMEM((2, SIDE, 2 * OWN, PACKED // 2), BF16),
            pltpu.VMEM((2, SIDE, 16, flat_half(MAIN)), BF16),
            pltpu.VMEM((2, SIDE, 16, flat_half(MAIN + LANES)), BF16),
            pltpu.VMEM((2, SIDE, 2 * OWN, PACKED // 2), BF16),
            pltpu.VMEM((2, SIDE, 16, flat_half(MAIN)), BF16),
            pltpu.VMEM((2, SIDE, 16, flat_half(MAIN + LANES)), BF16),
            dma((7,)),
            dma((2, SIDE * SIDE)),
            dma((2, SIDE * SIDE)),
        ]
        + [dma((2, SIDE))] * 6
        + [dma((2, 2, SIDE))] * 2
        + [pltpu.SemaphoreType.REGULAR] * 2,
        compiler_params=pltpu.CompilerParams(
            collective_id=0, has_side_effects=True, vmem_limit_bytes=40 * 1024 * 1024
        ),
    )(
        *[pltpu.with_memory_space_constraint(v, pltpu.HBM) for v in (
        jnp.transpose(latent, (1, 0, 2)),
        weight_one.reshape(27, OWN, chans),
        weight_two.reshape(27, OWN, chans),
        gain_one.reshape(1, OWN),
        bias_one.reshape(1, OWN),
        gain_two.reshape(1, OWN),
        bias_two.reshape(1, OWN),
    )]
    )
    return jnp.transpose(result, (1, 0, 2))


def solution(mesh):
    in_specs = (
        P("chan", "tm", None),
        P("chan"),
        P(None, None, "chan", None),
        P("chan"),
        P("chan"),
        P(None, None, "chan", None),
        P("chan"),
    )
    return jax.shard_map(
        functools.partial(block, mesh.shape["tm"]),
        mesh=mesh,
        in_specs=in_specs,
        out_specs=P("chan", "tm", None),
        check_vma=False,
    )
```

```python
import functools

import jax
import jax.numpy as jnp
from jax import lax
from jax.experimental import pallas as pl
from jax.experimental.pallas import tpu as pltpu
from jax.sharding import PartitionSpec as P

COLS = 104
ROWS = 4
LANES = 128
WIDE = ROWS * LANES
SIDE = 4
OWN = 24
FRAMES = 3
MAIN = 384
REST = ROWS * COLS - MAIN
PACKED = FRAMES * MAIN + LANES
DEPTH = 256
F32 = jnp.float32
BF16 = jnp.bfloat16


def unfold(value):
    value = value.astype(F32)
    return jnp.concatenate([value[:OWN], value[OWN:]], axis=1)


def fold(value):
    half = PACKED // 2
    return jnp.concatenate([value[:, :half], value[:, half:]], axis=0).astype(BF16)


def flat_half(width):
    return (OWN // 8 * width + LANES) // (2 * LANES) * LANES


def fold_next(value):
    width = value.shape[1]
    half = flat_half(width)
    parts = [value[8 * n : 8 * n + 8] for n in range(OWN // 8)]
    if 2 * half > OWN // 8 * width:
        parts.append(jnp.zeros((8, LANES), F32))
    flat = jnp.concatenate(parts, axis=1)
    return jnp.concatenate([flat[:, :half], flat[:, half:]], axis=0).astype(BF16)


def unfold_next(value, width):
    value = value.astype(F32)
    flat = jnp.concatenate([value[:8], value[8:]], axis=1)
    return jnp.concatenate([flat[:, width * n : width * (n + 1)] for n in range(OWN // 8)], axis=0)


def spread_lanes(value):
    return jnp.concatenate([value] * (PACKED // LANES), axis=1)


def lane_ids(rows):
    return lax.broadcasted_iota(jnp.int32, (rows, LANES), 1)


def tiles(value):
    return [value[:, n : n + LANES] for n in range(0, value.shape[1], LANES)]


def spread(packed, f):
    parts = tiles(packed)
    cells = parts[3 * f : 3 * f + 3] + [pltpu.roll(parts[-1], LANES - REST * f, 1) if f else parts[-1]]
    lane = lane_ids(OWN)
    rows = []
    for row in range(ROWS):
        at, off = divmod(row * COLS, LANES)
        piece = cells[at]
        if off:
            piece = jnp.where(
                lane < LANES - off,
                pltpu.roll(piece, LANES - off, 1),
                pltpu.roll(cells[at + 1], LANES - off, 1),
            )
        rows.append(jnp.where(lane < COLS, piece, 0.0))
    return rows


def pack(frame, place):
    rows = tiles(frame)
    lane = lane_ids(frame.shape[0])
    pieces = []
    for at in range(MAIN // LANES):
        row, off = divmod(at * LANES, COLS)
        piece = pltpu.roll(rows[row], LANES - off, 1) if off else rows[row]
        pieces.append(jnp.where(lane < COLS - off, piece, pltpu.roll(rows[row + 1], COLS - off, 1)))
    row, off = divmod(MAIN, COLS)
    return jnp.concatenate(pieces, axis=1), pltpu.roll(rows[row], (LANES - off + REST * place) % LANES, 1)


def join(packs):
    lane = lane_ids(packs[0][0].shape[0])
    rest = jnp.zeros(packs[0][1].shape, F32)
    for place in range(len(packs) - 1, -1, -1):
        rest = jnp.where(lane < REST * (place + 1), packs[place][1], rest)
    return jnp.concatenate([main for main, _ in packs] + [rest], axis=1)


def pack_latent(lat):
    packs = []
    for f in range(FRAMES):
        frame = lat[f].astype(F32)
        rest = jnp.concatenate([frame[:, MAIN:], jnp.zeros((OWN, LANES - REST), F32)], axis=1)
        packs.append((frame[:, :MAIN], pltpu.roll(rest, REST * f, 1) if f else rest))
    return join(packs)


def kernel(
    sections,
    chans,
    lat_hbm,
    w1_hbm,
    w2_hbm,
    g1_hbm,
    b1_hbm,
    g2_hbm,
    b2_hbm,
    out_ref,
    lat,
    weights,
    vecs,
    flipped,
    values,
    squares,
    partial_all,
    turned,
    w_out,
    w_in,
    stacked,
    sums,
    own_sums,
    shares,
    shares_far,
    shares_near,
    from_line,
    before_far,
    before_near,
    local_sem,
    all_send,
    all_recv,
    value_send,
    value_recv,
    w_send,
    w_recv,
    line_send,
    line_recv,
    next_send,
    next_recv,
    next_ready,
    ready,
):
    t = lax.axis_index("tm")
    chan = lax.axis_index("chan")
    x, y = lax.rem(chan, SIDE), lax.div(chan, SIDE)
    parity = lax.rem(t, 2)

    swap = [parity, 1 - parity]
    index_a = [x + s * (y - x) for s in swap]
    index_b = [y + s * (x - y) for s in swap]

    def chan_at(j, a, b):
        s = swap[j]
        return a * (1 + (SIDE - 1) * s) + b * (SIDE - (SIDE - 1) * s)

    def shifted(index, d):
        return lax.rem(index + d, SIDE)

    def a_peer(j, d):
        return (t, chan_at(j, shifted(index_a[j], d), index_b[j]))

    def b_peer(j, d, later=0):
        return (t + later, chan_at(j, index_a[j], shifted(index_b[j], d)))

    def remote(src, dst, send, recv, device):
        return pltpu.make_async_remote_copy(
            src_ref=src,
            dst_ref=dst,
            send_sem=send,
            recv_sem=recv,
            device_id=device,
            device_id_type=pl.DeviceIdType.MESH,
        )

    near, far, far_first, next_order = (1, 3), (2,), (1, 2, 3), (2, 1, 3, 0)

    loads = [
        pltpu.make_async_copy(lat_hbm, lat, local_sem.at[0]),
        pltpu.make_async_copy(w1_hbm, weights.at[0], local_sem.at[1]),
        pltpu.make_async_copy(w2_hbm, weights.at[1], local_sem.at[2]),
    ]
    for n, ref in enumerate((g1_hbm, b1_hbm, g2_hbm, b2_hbm)):
        loads.append(pltpu.make_async_copy(ref, vecs.at[n], local_sem.at[3 + n]))

    barrier = pltpu.get_barrier_semaphore()

    def tell(semaphore, device):
        pl.semaphore_signal(semaphore, inc=1, device_id=device, device_id_type=pl.DeviceIdType.MESH)

    def greet(device):
        tell(barrier, device)

    for d in far_first:
        greet((t, SIDE * y + shifted(x, d)))
        greet((t, SIDE * shifted(y, d) + x))

    @pl.when(t < sections - 1)
    def _():
        greet((t + 1, chan))

    for load in loads:
        load.start()

    def own_squares(value):
        sums_of = jnp.sum(value * value, axis=0, keepdims=True)
        for n, part in enumerate(tiles(sums_of)):
            squares[n : n + 1, :] = part

    for n in range(4):
        loads[3 + n].wait()
    flipped[...] = jnp.zeros((LANES, LANES), F32)
    for n in range(4):
        flipped[n : n + 1, 0:OWN] = vecs[n]
    columns = jnp.transpose(flipped[...])[:OWN]

    def column(n):
        return jnp.broadcast_to(columns[:, n : n + 1], (OWN, LANES))

    bias = [column(1), column(3)]
    gain = [spread_lanes(column(0)), spread_lanes(column(2))]

    squares[...] = jnp.zeros((16, LANES), F32)
    loads[0].wait()
    value = pack_latent(lat)
    values[0, 0] = fold(value * gain[0])
    own_squares(value)
    partial_all[0, 0] = squares[...].astype(BF16)

    sends = []

    def start(copy):
        copy.start()
        sends.append(copy)

    def drain():
        for copy in sends:
            copy.wait_send()
        sends.clear()

    def drain_next(j):
        @pl.when(t < sections - 1)
        def _():
            for e in range(SIDE):
                for part in range(2):
                    next_copy(j, e, part).wait_send()

    def send_values(j, steps):
        for d in steps:
            start(
                remote(
                    values.at[j, 0],
                    values.at[j, SIDE - d],
                    value_send.at[j, d],
                    value_recv.at[j, SIDE - d],
                    a_peer(j, d),
                )
            )

    def wait_values(j, slot):
        remote(
            values.at[j, 0], values.at[j, slot], value_send.at[j, slot], value_recv.at[j, slot], a_peer(j, slot)
        ).wait_recv()

    def any_copy(j, di, dj):
        to = (SIDE - di) % SIDE * SIDE + (SIDE - dj) % SIDE
        return remote(
            partial_all.at[j, 0],
            partial_all.at[j, to],
            all_send.at[j, di * SIDE + dj],
            all_recv.at[j, to],
            (t, SIDE * shifted(y, dj) + shifted(x, di)),
        )

    others = sorted(
        [(di, dj) for di in range(SIDE) for dj in range(SIDE) if di or dj],
        key=lambda o: -min(o[0], SIDE - o[0]) - min(o[1], SIDE - o[1]),
    )

    def send_squares(j, diagonal):
        for di, dj in others:
            if bool(di and dj) == diagonal:
                start(any_copy(j, di, dj))

    def scales_all(j):
        total = partial_all[j, 0].astype(F32)
        for di, dj in others[::-1]:
            any_copy(j, SIDE - di if di else 0, SIDE - dj if dj else 0).wait_recv()
            total = total + partial_all[j, di * SIDE + dj].astype(F32)
        return lax.rsqrt(total / chans + 1e-06)

    def turn_weights(j):
        loads[1 + j].wait()
        for k in range(3):
            part = weights[j, 9 * k : 9 * k + 9].astype(F32).reshape(9 * OWN, chans)
            part = jnp.concatenate([part, jnp.zeros((DEPTH - 9 * OWN, chans), F32)], axis=0)
            flat = jnp.transpose(part)
            turned[...] = flat
            for d in range(SIDE):
                rows = []
                for e in range(SIDE):
                    block = chan_at(j, shifted(index_a[j], d), shifted(index_b[j], e))
                    rows.append(turned[pl.ds(pl.multiple_of(block * OWN, 8), OWN), :])
                rows = jnp.concatenate(rows, axis=0).astype(BF16)
                if d == 0:
                    w_in[j, 0, k] = rows
                else:
                    w_out[j, d - 1, k] = rows

    def send_weights(j, steps):
        for d in steps:
            start(
                remote(
                    w_out.at[j, d - 1],
                    w_in.at[j, SIDE - d],
                    w_send.at[j, d],
                    w_recv.at[j, SIDE - d],
                    a_peer(j, d),
                )
            )

    def stack_taps(slot, j, scale):
        normed = unfold(values[j, slot]) * jnp.concatenate([scale[n : n + 1] for n in range(PACKED // LANES)], axis=1)
        act = 0.5 * normed * (1.0 + jnp.tanh(0.5 * normed))
        act = act.astype(BF16).astype(F32)
        for f in range(FRAMES):
            rows = spread(act, f)
            shifts = [
                [pltpu.roll(r, 1, 1) for r in rows],
                rows,
                [pltpu.roll(r, LANES - 1, 1) for r in rows],
            ]
            none = jnp.zeros((OWN, LANES), F32)
            taps = []
            for dy in range(3):
                for dx in range(3):
                    moved = [none] + shifts[dx] + [none]
                    taps.append(jnp.concatenate(moved[dy : dy + ROWS], axis=1))
            taps.append(jnp.zeros((DEPTH - 9 * OWN, WIDE), F32))
            stacked[f, slot] = jnp.concatenate(taps, axis=0).astype(BF16)

    group = SIDE * OWN

    def emit_all(j, product):
        last = product(2)
        main, rest = pack(last[:group], 1)
        for e in range(SIDE):
            shares_far[j, e] = fold_next(main[e * OWN : (e + 1) * OWN])

        @pl.when(t < sections - 1)
        def _():
            if j == 0:
                pl.semaphore_wait(next_ready, 1)
            for e in next_order:
                next_copy(j, e, 0).start()

        sums[2, :group] = last[group : 2 * group]
        sums[2, group : 2 * group] = last[2 * group :]
        mid = product(1)
        nearer, its_rest = pack(sums[2, :group] + mid[:group], 0)
        lane = lane_ids(group)
        rest = jnp.where(lane < REST, its_rest, jnp.where(lane < 2 * REST, rest, 0.0))
        nearer = jnp.concatenate([nearer, rest], axis=1)
        for e in range(SIDE):
            shares_near[j, e] = fold_next(nearer[e * OWN : (e + 1) * OWN])

        @pl.when(t < sections - 1)
        def _():
            for e in next_order:
                next_copy(j, e, 1).start()

        sums[2, group : 2 * group] += mid[group : 2 * group]
        sums[2, :group] = mid[2 * group :]
        first = product(0)
        frames = [
            first[2 * group :],
            sums[2, :group] + first[group : 2 * group],
            sums[2, group : 2 * group] + first[:group],
        ]
        packed = join([pack(frame, f) for f, frame in enumerate(frames)])
        own_sums[...] = packed[:OWN]
        for e in range(1, SIDE):
            shares[j, e] = fold(packed[e * OWN : (e + 1) * OWN])
        for d in far_first:
            start(line_copy(j, d))

    def left_of(j, slot):
        return w_in[j, slot].reshape(3 * group, DEPTH)

    def wait_weights(j, slot):
        remote(
            w_out.at[j, 0], w_in.at[j, slot], w_send.at[j, slot], w_recv.at[j, slot], a_peer(j, slot)
        ).wait_recv()

    def convolve_as_weights_come(j):
        for slot in (0, 2, 3):
            if slot:
                wait_weights(j, slot)
            for f in range(3):
                part = jnp.dot(left_of(j, slot), stacked[f, slot], preferred_element_type=F32)
                if slot:
                    part = part + sums[f]
                sums[f] = part
        wait_weights(j, 1)
        emit_all(j, lambda f: sums[f] + jnp.dot(left_of(j, 1), stacked[f, 1], preferred_element_type=F32))

    def convolve(j):
        for slot in (1, 3, 2):
            wait_weights(j, slot)
        left = jnp.concatenate([left_of(j, s) for s in range(SIDE)], axis=1)
        emit_all(
            j, lambda f: jnp.dot(left, stacked[f].reshape(SIDE * DEPTH, WIDE), preferred_element_type=F32)
        )

    def next_copy(j, e, part):
        return remote(
            (shares_far, shares_near)[part].at[j, e],
            (before_far, before_near)[part].at[j, e],
            next_send.at[j, part, e],
            next_recv.at[j, part, e],
            b_peer(j, e, 1),
        )

    def line_copy(j, d):
        return remote(
            shares.at[j, d],
            from_line.at[j, SIDE - d],
            line_send.at[j, d],
            line_recv.at[j, SIDE - d],
            b_peer(j, d),
        )

    def collect(j):
        @pl.when(t > 0)
        def _():
            for part, landed in enumerate((before_far, before_near)):
                for e in range(SIDE):
                    remote(
                        landed.at[j, e],
                        landed.at[j, e],
                        next_send.at[j, part, e],
                        next_recv.at[j, part, e],
                        (t, chan_at(j, shifted(index_a[j], 1), index_b[j])),
                    ).wait_recv()

        for d in (1, 3, 2):
            remote(
                from_line.at[j, d],
                from_line.at[j, d],
                line_send.at[j, d],
                line_recv.at[j, d],
                b_peer(j, d),
            ).wait_recv()
        total = own_sums[...] + spread_lanes(bias[j])
        for d in range(1, SIDE):
            total = total + unfold(from_line[j, d])
        second = unfold_next(before_far[j, 0], MAIN)
        first = unfold_next(before_near[j, 0], MAIN + LANES)
        for e in range(1, SIDE):
            second = second + unfold_next(before_far[j, e], MAIN)
            first = first + unfold_next(before_near[j, e], MAIN + LANES)
        return jnp.concatenate(
            [
                total[:, :MAIN] + first[:, :MAIN],
                total[:, MAIN : 2 * MAIN] + second,
                total[:, 2 * MAIN : 3 * MAIN],
                total[:, 3 * MAIN :] + first[:, MAIN:],
            ],
            axis=1,
        )

    @pl.when(t == 0)
    def _():
        before_far[...] = jnp.zeros(before_far.shape, BF16)
        before_near[...] = jnp.zeros(before_near.shape, BF16)

    pl.semaphore_wait(barrier, 6 + jnp.where(t > 0, 1, 0))
    for d in (1, 2, 3):
        tell(ready, (t, SIDE * y + shifted(x, d)))
    send_squares(0, False)
    send_values(0, far_first)
    turn_weights(0)
    send_weights(0, far)
    pl.semaphore_wait(ready, 3)
    send_squares(0, True)
    send_weights(0, near)

    @pl.when(t > 0)
    def _():
        tell(next_ready, (t - 1, chan))

    turn_weights(1)
    scale = scales_all(0)
    for slot in (0, 1, 3, 2):
        if slot:
            wait_values(0, slot)
        stack_taps(slot, 0, scale)
    early = list(sends)
    sends.clear()
    convolve_as_weights_come(0)
    send_weights(1, far_first)

    middle = collect(0)
    rest = jnp.where(lane_ids(OWN) < FRAMES * REST, middle[:, FRAMES * MAIN :], 0.0)
    middle = jnp.concatenate([middle[:, : FRAMES * MAIN], rest], axis=1).astype(BF16).astype(F32)
    values[1, 0] = fold(middle * gain[1])
    own_squares(middle)
    partial_all[1, 0] = squares[...].astype(BF16)
    send_squares(1, False)
    send_squares(1, True)
    send_values(1, far_first)
    for copy in early:
        copy.wait_send()
    scale = scales_all(1)
    for slot in (0, 1, 3, 2):
        if slot:
            wait_values(1, slot)
        stack_taps(slot, 1, scale)
    middle_sends = list(sends)
    sends.clear()
    convolve(1)
    for copy in middle_sends:
        copy.wait_send()
    drain_next(0)
    result = pack_latent(lat) + collect(1)
    for f in range(FRAMES):
        rest = result[:, FRAMES * MAIN :]
        rest = pltpu.roll(rest, LANES - REST * f, 1) if f else rest
        frame = jnp.concatenate([result[:, f * MAIN : (f + 1) * MAIN], rest], axis=1)
        out_ref[f] = frame[:, : ROWS * COLS].astype(BF16)

    drain()
    drain_next(1)


def block(sections, latent, gain_one, weight_one, bias_one, gain_two, weight_two, bias_two):
    frames = latent.shape[1]
    chans = weight_one.shape[3]
    dma = pltpu.SemaphoreType.DMA
    anywhere = pl.BlockSpec(memory_space=pltpu.HBM)
    result = pl.pallas_call(
        functools.partial(kernel, sections, chans),
        out_shape=jax.ShapeDtypeStruct((frames, OWN, ROWS * COLS), BF16),
        in_specs=[anywhere] * 7,
        out_specs=pl.BlockSpec(memory_space=pltpu.VMEM),
        scratch_shapes=[
            pltpu.VMEM((frames, OWN, ROWS * COLS), BF16),
            pltpu.VMEM((2, 27, OWN, chans), BF16),
            pltpu.VMEM((4, 1, OWN), F32),
            pltpu.VMEM((LANES, LANES), F32),
            pltpu.VMEM((2, SIDE, 2 * OWN, PACKED // 2), BF16),
            pltpu.VMEM((16, LANES), F32),
            pltpu.VMEM((2, SIDE * SIDE, 16, LANES), BF16),
            pltpu.VMEM((chans, DEPTH), F32),
            pltpu.VMEM((2, SIDE - 1, 3, SIDE * OWN, DEPTH), BF16),
            pltpu.VMEM((2, SIDE, 3, SIDE * OWN, DEPTH), BF16),
            pltpu.VMEM((frames, SIDE, DEPTH, WIDE), BF16),
            pltpu.VMEM((frames, 3 * SIDE * OWN, WIDE), F32),
            pltpu.VMEM((OWN, PACKED), F32),
            pltpu.VMEM((2, SIDE, 2 * OWN, PACKED // 2), BF16),
            pltpu.VMEM((2, SIDE, 16, flat_half(MAIN)), BF16),
            pltpu.VMEM((2, SIDE, 16, flat_half(MAIN + LANES)), BF16),
            pltpu.VMEM((2, SIDE, 2 * OWN, PACKED // 2), BF16),
            pltpu.VMEM((2, SIDE, 16, flat_half(MAIN)), BF16),
            pltpu.VMEM((2, SIDE, 16, flat_half(MAIN + LANES)), BF16),
            dma((7,)),
            dma((2, SIDE * SIDE)),
            dma((2, SIDE * SIDE)),
        ]
        + [dma((2, SIDE))] * 6
        + [dma((2, 2, SIDE))] * 2
        + [pltpu.SemaphoreType.REGULAR] * 2,
        compiler_params=pltpu.CompilerParams(
            collective_id=0, has_side_effects=True, vmem_limit_bytes=40 * 1024 * 1024
        ),
    )(
        *[pltpu.with_memory_space_constraint(v, pltpu.HBM) for v in (
        jnp.transpose(latent, (1, 0, 2)),
        weight_one.reshape(27, OWN, chans),
        weight_two.reshape(27, OWN, chans),
        gain_one.reshape(1, OWN),
        bias_one.reshape(1, OWN),
        gain_two.reshape(1, OWN),
        bias_two.reshape(1, OWN),
    )]
    )
    return jnp.transpose(result, (1, 0, 2))


def solution(mesh):
    in_specs = (
        P("chan", "tm", None),
        P("chan"),
        P(None, None, "chan", None),
        P("chan"),
        P("chan"),
        P(None, None, "chan", None),
        P("chan"),
    )
    return jax.shard_map(
        functools.partial(block, mesh.shape["tm"]),
        mesh=mesh,
        in_specs=in_specs,
        out_specs=P("chan", "tm", None),
        check_vma=False,
    )
```
